512 devices in a mesh: gx: 64 (over x, y, z_lo), gy: 8 (over z_hi, core).
Axes of the slice: x: 4, y: 8, z: 8 (z_hi: 4, z_lo: 2; z = z_hi * 2 + z_lo), core: 2. Of those that a mesh axis runs over, the one named last changes fastest.
Arguments:
- hidden_in: bfloat16 [10, 16384], P(None, 'gx'), may hold values from -4000 to 4000
- norm_gain: bfloat16 [16384], P('gx'), may hold values from 0.099609375 to 1.8984375
- w_query: bfloat16 [16384, 16384], P('gx', 'gy'), may hold values from -0.046875 to 0.046875
- w_keyval: bfloat16 [16384, 2048], P('gx', 'gy'), may hold values from -0.09375 to 0.09375
- w_output: bfloat16 [16384, 16384], P('gx', 'gy'), may hold values from -0.1875 to 0.1875
- key_cache: bfloat16 [10, 8, 32768, 128], P(None, 'gy', 'gx'), may hold values from -1100 to 1100
- value_cache: bfloat16 [10, 8, 32768, 128], P(None, 'gy', 'gx'), may hold values from -6 to 6
- lengths: int32 [10], replicated, may hold values from 1 to 32768, as said below
Outputs:
- attn_out: bfloat16 [10, 16384], P(None, 'gy')
The draws below stay inside these ranges and needn't reach their ends.
Inputs may be any that keep to these rules, and one draw needn't show every extreme that they name: `lengths`: some row holds 32768 positions.
All inputs are finite; a program needn't handle non-finite values.
Results may differ from the reference program's by a relative error of at most 0.012.
The reference program's roundings to bfloat16 on the way (of `scaled_in`, `query_new`, `keyval_new`, `weights` and `attention`) count: a program that leaves them out, or rounds other values in their place, can miss the bound.
Values may be sent and summed in bfloat16 or wider, within the bound.
A program may use at most 64 MiB of HBM per device.

```python
import jax
import jax.numpy as jnp
from jax import lax

D = 16384
HEADS = 128
KV = 8
HD = 128
CTX = 32768
ROWS = 10


def draw_hidden_in(key, part):
    key = jax.random.fold_in(key, 11)
    first_key, second_key = jax.random.split(key, 2)
    row_scale = 10.0 ** jax.random.uniform(second_key, (ROWS, 1), dtype=jnp.float32)
    col_scale = 10.0 ** (jnp.arange(D, dtype=jnp.float32)[None, :] / D)
    values = jax.random.normal(first_key, (ROWS, D), dtype=jnp.float32) * row_scale * col_scale
    return jnp.clip(values, -4000.0, 4000.0).astype(jnp.bfloat16)


def draw_key_cache(key, part):
    key = jax.random.fold_in(key, 23)
    first_key = jax.random.fold_in(key, 0)
    values = 2.0 * jax.random.normal(first_key, (ROWS, KV, CTX, HD), dtype=jnp.float32)
    return jnp.clip(values, -1100.0, 1100.0).astype(jnp.bfloat16)


def draw_lengths(key, part):
    key = jax.random.fold_in(key, 37)
    first_key, second_key, third_key = jax.random.split(key, 3)
    bit_count = CTX.bit_length() - 1
    exponent = jax.random.randint(first_key, (ROWS,), 0, bit_count + 1)
    upper_bound = jnp.left_shift(jnp.ones((ROWS,), jnp.int32), exponent)
    drawn = 1 + jax.random.randint(second_key, (ROWS,), 0, upper_bound)
    drawn = jnp.minimum(drawn, CTX)
    longest = jax.random.randint(third_key, (), 0, ROWS)
    return jnp.where(jnp.arange(ROWS, dtype=jnp.int32) == longest, CTX, drawn).astype(jnp.int32)


def level_of(key, dims, cuts, smallest, largest):
    def one(dim, shards_of):
        steps = jax.random.uniform(jax.random.fold_in(jax.random.fold_in(key, 6), dim), (shards_of,), jnp.float32, smallest / len(cuts), largest / len(cuts))
        return jnp.repeat(jnp.exp(steps), dims[dim] // shards_of).reshape((-1,) + (1,) * (len(dims) - dim - 1))

    level = one(*cuts[0])
    for cut in cuts[1:]:
        level = level * one(*cut)
    return level


def normal_values(rng, shape, scale, reach, shards=(), kind=jnp.bfloat16):
    values = scale * jax.random.normal(rng, shape, jnp.float32)
    if shards:
        values = values * level_of(rng, shape, shards, -0.22, 0.18)
    return jnp.clip(values, -reach, reach).astype(kind)


def setup_inputs(seed: int = 0) -> dict:
    streams_of = jax.random.split(jax.random.key(seed), 9)
    return {
        "hidden_in": draw_hidden_in(jax.random.fold_in(streams_of[8], 71), 0),
        "norm_gain": jnp.clip(1.0 + 0.18 * jax.random.normal(streams_of[1], (D,), jnp.float32), 0.099609375, 1.8984375).astype(jnp.bfloat16),
        "w_query": normal_values(streams_of[2], (D, HEADS * HD), D ** -0.5, 0.046875, ((0, 64), (1, 8))),
        "w_keyval": normal_values(streams_of[3], (D, 2 * KV * HD), (D // 4) ** -0.5, 0.09375, ((0, 64), (1, 8))),
        "w_output": normal_values(streams_of[4], (HEADS * HD, D), (HEADS * HD // 16) ** -0.5, 0.1875, ((0, 64), (1, 8))),
        "key_cache": draw_key_cache(jax.random.fold_in(streams_of[8], 71), 0),
        "value_cache": normal_values(streams_of[6], (ROWS, KV, CTX, HD), 1.0, 6.0, ((1, 8), (2, 64))),
        "lengths": draw_lengths(jax.random.fold_in(streams_of[8], 71), 0),
    }


def reference(hidden_in, norm_gain, w_query, w_keyval, w_output, key_cache, value_cache, lengths):
    hidden_f32 = hidden_in.astype(jnp.float32)
    inv_rms = lax.rsqrt(lax.optimization_barrier(jnp.mean(hidden_f32 * hidden_f32, axis=1, keepdims=True)) + 1e-05)
    scaled_in = (hidden_f32 * norm_gain.astype(jnp.float32)).astype(jnp.bfloat16)
    query_new = (jnp.dot(scaled_in, w_query, preferred_element_type=jnp.float32) * inv_rms).astype(jnp.bfloat16)
    query_new = query_new.reshape(ROWS, KV, HEADS // KV, HD)
    keyval_new = (jnp.dot(scaled_in, w_keyval, preferred_element_type=jnp.float32) * inv_rms).astype(jnp.bfloat16)
    keyval_new = keyval_new.reshape(ROWS, KV, 2, HD)
    score_scale = HD ** (-0.5)
    valid_pos = (jnp.arange(CTX, dtype=jnp.int32)[None, :] < lengths[:, None])[:, None, :]

    def one_head(head):
        query_head = query_new[:, head].astype(jnp.float32)
        key_head = lax.dynamic_index_in_dim(key_cache, head, 1, keepdims=False).astype(jnp.float32)
        value_head = lax.dynamic_index_in_dim(value_cache, head, 1, keepdims=False).astype(jnp.float32)
        key_fresh = keyval_new[:, head, 0].astype(jnp.float32)
        value_fresh = keyval_new[:, head, 1].astype(jnp.float32)
        score_new = lax.optimization_barrier(jnp.sum(query_head * key_fresh[:, None, :], axis=2)) * score_scale
        scores = jnp.einsum('bgd,bsd->bgs', query_head, key_head, precision=lax.Precision.HIGHEST) * score_scale
        top_score = jnp.maximum(lax.optimization_barrier(jnp.max(jnp.where(valid_pos, scores, -1e+30), axis=2)), score_new)
        weights = jnp.where(valid_pos, jnp.exp(jnp.where(valid_pos, scores, -1e+30) - top_score[..., None]), 0.0)
        fresh_weight = jnp.exp(score_new - top_score)
        denominator = lax.optimization_barrier(jnp.sum(weights, axis=2)) + fresh_weight
        rounded = lax.optimization_barrier(weights.astype(jnp.bfloat16)).astype(jnp.float32)
        numerator = jnp.einsum('bgs,bsd->bgd', rounded, value_head, precision=lax.Precision.HIGHEST)
        numerator = numerator + fresh_weight[..., None] * value_fresh[:, None, :]
        return (numerator / denominator[..., None]).astype(jnp.bfloat16)
    attn_heads = lax.map(one_head, jnp.arange(KV, dtype=jnp.int32))
    attention = jnp.transpose(attn_heads, (1, 0, 2, 3)).reshape(ROWS, HEADS * HD)
    return jnp.dot(attention, w_output, preferred_element_type=jnp.float32).astype(jnp.bfloat16)
```

```python
import functools

import jax
import jax.numpy as jnp
from jax import lax
from jax.experimental import pallas as pl
from jax.experimental.pallas import tpu as pltpu
from jax.sharding import PartitionSpec as P

D = 16384
HEADS = 128
KV = 8
HD = 128
ROWS = 10
GROUP = HEADS // KV
SPAN = 512
NX = 64
NY = 8
MESH = pl.DeviceIdType.MESH

Q_UNITS = ROWS * GROUP
KEY_UNIT = Q_UNITS
VALUE_UNIT = KEY_UNIT + ROWS
SQUARE_UNIT = VALUE_UNIT + ROWS
IN_BLOCKS = (SQUARE_UNIT + ROWS + 3) // 4
OUT_BLOCKS = Q_UNITS // 4
HALF = ROWS // 2


def offset(index, size):
    return size // 2 + (1 - 2 * (index % 2)) * ((index + 1) // 2)


def peer(index, gx):
    dy, dx, dz = offset(index // 8, 8), offset((index // 2) % 4, 4), 1 - index % 2
    x, y, z = gx // 16, (gx // 2) % 8, gx % 2
    return ((x + dx) % 4) * 16 + ((y + dy) % 8) * 2 + (z + dz) % 2


def put_unit(ref, unit, value):
    ref[unit // 4, pl.ds(unit % 4, 1), :] = value


def await_bytes(ref, sem):
    pltpu.make_async_copy(ref, ref, sem).wait()


def kernel(
    hidden_ref, gain_ref, w_query_hbm, w_keyval_hbm, w_output_hbm, key_hbm, value_hbm, lengths_ref,
    out_ref,
    w_query, w_keyval, w_output, keys, values,
    in_send, in_recv, in_sum, in_all,
    soft_send, soft_recv, attn_send, attn_recv,
    out_send, out_recv, out_sum,
    load_sem, send_sem, recv_sem,
):
    gx, gy = lax.axis_index("gx"), lax.axis_index("gy")
    merges = (gx // 8) % 2 == gy % 2
    soft_block = (2 * (gx % 8) + gx // 32) * 2 + (gx // 16) % 2
    attn_gx = gy * 8 + gx % 8
    home = gx // 8

    barrier = pltpu.get_barrier_semaphore()

    def greet(index, carry):
        pl.semaphore_signal(barrier, inc=1, device_id=(peer(index, gx), gy), device_id_type=MESH)
        return carry

    lax.fori_loop(0, NX - 1, greet, 0)

    @pl.when(gy != home)
    def _():
        def greet_merger(index, carry):
            merger = index * 16 + (home % 2) * 8 + gx % 8
            pl.semaphore_signal(barrier, inc=1, device_id=(merger, home), device_id_type=MESH)
            return carry

        lax.fori_loop(0, 4, greet_merger, 0)

    loads = [
        pltpu.make_async_copy(src, dst, load_sem.at[k])
        for k, (src, dst) in enumerate(
            [
                (w_query_hbm, w_query),
                (w_keyval_hbm, w_keyval),
                (key_hbm, keys),
                (value_hbm, values),
                (w_output_hbm, w_output),
            ]
        )
    ]
    for load in loads:
        load.start()

    def reduce_blocks(stage, blocks, send, recv, total):
        mine = gx < blocks

        def send_block(index, carry):
            target = peer(index, gx)

            @pl.when(target < blocks)
            def _():
                pltpu.make_async_remote_copy(
                    src_ref=send.at[target], dst_ref=recv.at[gx],
                    send_sem=send_sem.at[stage], recv_sem=recv_sem.at[stage],
                    device_id=(target, gy), device_id_type=MESH,
                ).start()

            return carry

        lax.fori_loop(0, NX - 1, send_block, 0)

        @pl.when(mine)
        def _():
            recv[gx] = send[gx]
            await_bytes(recv.at[pl.ds(0, NX - 1)], recv_sem.at[stage])
            total[...] = jnp.sum(recv[...], axis=0)

    def spread_blocks(stage, blocks, total, everything):
        mine = gx < blocks

        @pl.when(mine)
        def _():
            def send_total(index, carry):
                pltpu.make_async_remote_copy(
                    src_ref=total, dst_ref=everything.at[gx],
                    send_sem=send_sem.at[stage], recv_sem=recv_sem.at[stage],
                    device_id=(peer(index, gx), gy), device_id_type=MESH,
                ).start()
                return carry

            lax.fori_loop(0, NX - 1, send_total, 0)
            everything[gx] = total[...]
            await_bytes(everything.at[pl.ds(0, blocks - 1)], recv_sem.at[stage])

        @pl.when(jnp.logical_not(mine))
        def _():
            await_bytes(everything.at[pl.ds(0, blocks)], recv_sem.at[stage])

    hidden = hidden_ref[...].astype(jnp.float32)
    squares = jnp.broadcast_to(jnp.sum(hidden * hidden, axis=1, keepdims=True), (ROWS, HD))
    scaled_in = (hidden * gain_ref[...].astype(jnp.float32)).astype(jnp.bfloat16)
    loads[0].wait()
    query_part = jnp.dot(scaled_in, w_query[...], preferred_element_type=jnp.float32)
    for r in range(ROWS):
        for h in range(GROUP):
            put_unit(in_send, r * GROUP + h, query_part[r : r + 1, h * HD : (h + 1) * HD])
    loads[1].wait()
    keyval_part = jnp.dot(scaled_in, w_keyval[...], preferred_element_type=jnp.float32)
    for r in range(ROWS):
        put_unit(in_send, KEY_UNIT + r, keyval_part[r : r + 1, :HD])
        put_unit(in_send, VALUE_UNIT + r, keyval_part[r : r + 1, HD:])
        put_unit(in_send, SQUARE_UNIT + r, squares[r : r + 1])
    for unit in range(SQUARE_UNIT + ROWS, IN_BLOCKS * 4):
        put_unit(in_send, unit, jnp.zeros((1, HD), jnp.float32))

    @pl.when(merges)
    def _():
        pl.semaphore_wait(barrier, NX - 1 + NY - 1)

    @pl.when(jnp.logical_not(merges))
    def _():
        pl.semaphore_wait(barrier, NX - 1)

    reduce_blocks(0, IN_BLOCKS, in_send, in_recv, in_sum)
    spread_blocks(1, IN_BLOCKS, in_sum, in_all)

    def unit(index):
        return in_all[index // 4, index % 4 : index % 4 + 1, :]

    loads[2].wait()
    loads[3].wait()
    score_scale = HD ** (-0.5)
    position = gx * SPAN + lax.broadcasted_iota(jnp.int32, (GROUP, SPAN), 1)
    lane = lax.broadcasted_iota(jnp.int32, (GROUP, HD), 1)
    first = gx == 0
    for half in range(2):
        peaks = jnp.zeros((GROUP, HD), jnp.float32)
        totals = jnp.zeros((GROUP, HD), jnp.float32)
        for k in range(HALF):
            r = half * HALF + k
            inv_rms = lax.rsqrt(unit(SQUARE_UNIT + r) / D + 1e-05)
            query = in_all[r * 4 : r * 4 + 4].reshape(GROUP, HD)
            query = (query * inv_rms).astype(jnp.bfloat16)
            key_new = (unit(KEY_UNIT + r) * inv_rms).astype(jnp.bfloat16).astype(jnp.float32)
            value_new = (unit(VALUE_UNIT + r) * inv_rms).astype(jnp.bfloat16).astype(jnp.float32)
            score_new = (
                jnp.sum(query.astype(jnp.float32) * key_new, axis=1, keepdims=True) * score_scale
            )
            score_new = jnp.where(first, score_new, -1e30)
            scores = (
                lax.dot_general(
                    query, keys[r, 0], (((1,), (1,)), ((), ())), preferred_element_type=jnp.float32
                )
                * score_scale
            )
            valid = position < lengths_ref[r]
            masked = jnp.where(valid, scores, -1e30)
            peak = jnp.maximum(jnp.max(masked, axis=1, keepdims=True), score_new)
            weights = jnp.where(valid, jnp.exp(masked - peak), 0.0)
            fresh = jnp.where(first, jnp.exp(score_new - peak), 0.0)
            total = jnp.sum(weights, axis=1, keepdims=True) + fresh
            accum = jnp.dot(
                weights.astype(jnp.bfloat16), values[r, 0], preferred_element_type=jnp.float32
            )
            accum = accum + fresh * value_new
            for h in range(GROUP):
                soft_send[h * 2 + half, k : k + 1, :] = accum[h : h + 1]
            peaks = jnp.where(lane == k, peak, peaks)
            totals = jnp.where(lane == k, total, totals)
        for h in range(GROUP):
            soft_send[h * 2 + half, HALF : HALF + 1, :] = peaks[h : h + 1]
            soft_send[h * 2 + half, HALF + 1 : HALF + 2, :] = totals[h : h + 1]
            soft_send[h * 2 + half, HALF + 2 : HALF + 3, :] = jnp.zeros((1, HD), jnp.float32)

    def send_soft(index, carry):
        target = peer(index, gx)

        @pl.when((target // 8) % 2 == gy % 2)
        def _():
            block = (2 * (target % 8) + target // 32) * 2 + (target // 16) % 2
            pltpu.make_async_remote_copy(
                src_ref=soft_send.at[block], dst_ref=soft_recv.at[gx],
                send_sem=send_sem.at[2], recv_sem=recv_sem.at[2],
                device_id=(target, gy), device_id_type=MESH,
            ).start()

        return carry

    lax.fori_loop(0, NX - 1, send_soft, 0)

    @pl.when(merges)
    def _():
        soft_recv[gx] = soft_send[soft_block]
        await_bytes(soft_recv.at[pl.ds(0, NX - 1)], recv_sem.at[2])
        peaks = soft_recv[:, HALF, :]
        factors = jnp.exp(peaks - jnp.max(peaks, axis=0, keepdims=True))
        totals = jnp.sum(factors * soft_recv[:, HALF + 1, :], axis=0, keepdims=True)
        for k in range(HALF):
            weighted = jnp.sum(factors[:, k : k + 1] * soft_recv[:, k, :], axis=0, keepdims=True)
            attention = (weighted / totals[:, k : k + 1]).astype(jnp.bfloat16)
            attn_send[k : k + 1, :] = attention.astype(jnp.float32)
        attn_send[HALF:, :] = jnp.zeros((8 - HALF, HD), jnp.float32)

        def send_attention(index, carry):
            column = (gy + 4 + index) % NY

            @pl.when((column != gy) | (attn_gx != gx))
            def _():
                pltpu.make_async_remote_copy(
                    src_ref=attn_send, dst_ref=attn_recv.at[gx // 16],
                    send_sem=send_sem.at[3], recv_sem=recv_sem.at[3],
                    device_id=(attn_gx, column), device_id_type=MESH,
                ).start()

            return carry

        lax.fori_loop(0, NY, send_attention, 0)

    @pl.when(gy == home)
    def _():
        attn_recv[gx // 16] = attn_send[...]
        await_bytes(attn_recv.at[pl.ds(0, 3)], recv_sem.at[3])

    @pl.when(gy != home)
    def _():
        await_bytes(attn_recv, recv_sem.at[3])

    loads[4].wait()
    attention = jnp.concatenate(
        [
            jnp.concatenate([attn_recv[half], attn_recv[2 + half]], axis=1)
            for half in range(2)
        ],
        axis=0,
    ).astype(jnp.bfloat16)
    out_part = jnp.dot(attention, w_output[...], preferred_element_type=jnp.float32)
    for r in range(ROWS):
        row = r // HALF * 8 + r % HALF
        for c in range(GROUP):
            put_unit(out_send, r * GROUP + c, out_part[row : row + 1, c * HD : (c + 1) * HD])
    reduce_blocks(4, OUT_BLOCKS, out_send, out_recv, out_sum)
    spread_blocks(5, OUT_BLOCKS, out_sum, out_ref)

    def await_sends(stage, sender, ref, count):
        @pl.when(sender)
        def _():
            await_bytes(ref.at[pl.ds(0, count)], send_sem.at[stage])

    await_sends(0, gx < IN_BLOCKS, in_recv, IN_BLOCKS - 1)
    await_sends(0, gx >= IN_BLOCKS, in_recv, IN_BLOCKS)
    await_sends(1, gx < IN_BLOCKS, in_recv, NX - 1)
    await_sends(2, merges, soft_recv, 31)
    await_sends(2, jnp.logical_not(merges), soft_recv, 32)
    await_sends(3, merges & (attn_gx == gx), soft_recv, NY - 1)
    await_sends(3, merges & (attn_gx != gx), soft_recv, NY)
    await_sends(4, gx < OUT_BLOCKS, in_recv, OUT_BLOCKS - 1)
    await_sends(4, gx >= OUT_BLOCKS, in_recv, OUT_BLOCKS)
    await_sends(5, gx < OUT_BLOCKS, in_recv, NX - 1)


def per_device(hidden_in, norm_gain, w_query, w_keyval, w_output, key_cache, value_cache, lengths):
    vmem = pl.BlockSpec(memory_space=pltpu.VMEM)
    hbm = pl.BlockSpec(memory_space=pl.ANY)
    block = (4, HD)
    scratch = [
        pltpu.VMEM(w_query.shape, jnp.bfloat16),
        pltpu.VMEM(w_keyval.shape, jnp.bfloat16),
        pltpu.VMEM(w_output.shape, jnp.bfloat16),
        pltpu.VMEM(key_cache.shape, jnp.bfloat16),
        pltpu.VMEM(value_cache.shape, jnp.bfloat16),
        pltpu.VMEM((IN_BLOCKS, *block), jnp.float32),
        pltpu.VMEM((NX, *block), jnp.float32),
        pltpu.VMEM(block, jnp.float32),
        pltpu.VMEM((IN_BLOCKS, *block), jnp.float32),
        pltpu.VMEM((2 * GROUP, 8, HD), jnp.float32),
        pltpu.VMEM((NX, 8, HD), jnp.float32),
        pltpu.VMEM((8, HD), jnp.float32),
        pltpu.VMEM((4, 8, HD), jnp.float32),
        pltpu.VMEM((OUT_BLOCKS, *block), jnp.float32),
        pltpu.VMEM((NX, *block), jnp.float32),
        pltpu.VMEM(block, jnp.float32),
        pltpu.SemaphoreType.DMA((5,)),
        pltpu.SemaphoreType.DMA((6,)),
        pltpu.SemaphoreType.DMA((6,)),
    ]
    out = pl.pallas_call(
        kernel,
        out_shape=jax.ShapeDtypeStruct((OUT_BLOCKS, *block), jnp.float32),
        in_specs=[vmem, vmem, hbm, hbm, hbm, hbm, hbm, pl.BlockSpec(memory_space=pltpu.SMEM)],
        out_specs=vmem,
        scratch_shapes=scratch,
        compiler_params=pltpu.CompilerParams(
            collective_id=0, has_side_effects=True, vmem_limit_bytes=60 * 2**20
        ),
        cost_estimate=pl.CostEstimate(flops=64 * 2**20, bytes_accessed=5 * 2**20, transcendentals=81920),
    )(hidden_in, norm_gain.reshape(1, -1), w_query, w_keyval, w_output, key_cache, value_cache, lengths)
    return out.reshape(ROWS, GROUP * HD).astype(jnp.bfloat16)


def solution(mesh):
    return jax.shard_map(
        per_device,
        mesh=mesh,
        in_specs=(
            P(None, "gx"),
            P("gx"),
            P("gx", "gy"),
            P("gx", "gy"),
            P("gx", "gy"),
            P(None, "gy", "gx", None),
            P(None, "gy", "gx", None),
            P(),
        ),
        out_specs=P(None, "gy"),
        check_vma=False,
    )
```

```python
import jax
import jax.numpy as jnp
from jax import lax
from jax.experimental import pallas as pl
from jax.experimental.pallas import tpu as pltpu
from jax.sharding import PartitionSpec as P

D = 16384
HEADS = 128
KV = 8
HD = 128
ROWS = 10
GROUP = HEADS // KV
SPAN = 512
MESH = pl.DeviceIdType.MESH

SLICES = 8
PAIR = 2 * ROWS
BLOCK = PAIR + 4
PEAK = PAIR
TOTAL = PAIR + 1


def offset(index, size):
    return size // 2 + (1 - 2 * (index % 2)) * ((index + 1) // 2)


def await_bytes(ref, sem):
    pltpu.make_async_copy(ref, ref, sem).wait()


def merge_partials(blocks, count):
    peaks = blocks[:, PEAK, :]
    peak = jnp.max(peaks, axis=0, keepdims=True)
    factors = jnp.exp(peaks - peak)
    total = jnp.sum(factors * blocks[:, TOTAL, :], axis=0, keepdims=True)
    if count < 8:
        factors = jnp.concatenate([factors, jnp.broadcast_to(total, (8 - count, HD))], axis=0)
    columns = jnp.transpose(factors)
    accum = columns[:BLOCK, 0:1] * blocks[0]
    for k in range(1, count):
        accum = accum + columns[:BLOCK, k : k + 1] * blocks[k]
    return accum, peak, total, columns


def kernel(
    hidden_hbm, gain_hbm, w_query_hbm, w_keyval_hbm, w_output_hbm, key_hbm, value_hbm, lengths_ref,
    out_ref,
    hidden_in, norm_gain, w_query, w_keyval, w_output, keys, values,
    in_send, in_plane, in_mid, in_line, in_sum, in_all,
    soft_send, soft_recv, soft_mid, attn_recv,
    out_send, out_plane, out_mid, out_line, out_sum, out_all,
    load_sem, send_sem, recv_sem,
):
    gx, gy = lax.axis_index("gx"), lax.axis_index("gy")
    x, y, z = gx // 16, (gx // 2) % 8, gx % 2
    plane = x * 2 + z
    merges = y // 4 == gy % 2
    source_gy = 2 * x + y // 4

    def place(x, y, z):
        return x * 16 + y * 2 + z

    def plane_mate(index):
        return (x + offset(index // 2, 4)) % 4, (z + 1 - index % 2) % 2

    def line_mate(index):
        return (y + offset(index, 8)) % 8

    barrier = pltpu.get_barrier_semaphore()

    def signal(gx_to, gy_to):
        pl.semaphore_signal(barrier, inc=1, device_id=(gx_to, gy_to), device_id_type=MESH)

    @pl.when(source_gy != gy)
    def _():
        def greet_source(index, carry):
            signal(place(index, y, z), source_gy)
            return carry

        lax.fori_loop(0, 4, greet_source, 0)

    def greet(index, carry):
        x_mate, z_mate = plane_mate(index)
        y_mate = line_mate(index)
        signal(place(x, y_mate, 1 - z), gy)
        signal(place(x, y_mate, z), gy)
        signal(place(x_mate, y, z_mate), gy)
        return carry

    lax.fori_loop(0, 7, greet, 0)

    loads = [
        pltpu.make_async_copy(src, dst, load_sem.at[k])
        for k, (src, dst) in enumerate(
            [
                (hidden_hbm, hidden_in),
                (gain_hbm, norm_gain),
                (w_query_hbm, w_query),
                (w_keyval_hbm, w_keyval),
                (key_hbm, keys),
                (value_hbm, values),
                (w_output_hbm, w_output),
            ]
        )
    ]
    for load in loads:
        load.start()

    def copy(stage, src, dst, gx_to, gy_to):
        pltpu.make_async_remote_copy(
            src_ref=src, dst_ref=dst, send_sem=send_sem.at[stage], recv_sem=recv_sem.at[stage],
            device_id=(gx_to, gy_to), device_id_type=MESH,
        ).start()

    def all_reduce(stage, send, by_plane, mid, by_line, total, everything):
        def to_plane(index, carry):
            x_mate, z_mate = plane_mate(index)
            copy(stage, send.at[x_mate * 2 + z_mate], by_plane.at[plane], place(x_mate, y, z_mate), gy)
            return carry

        lax.fori_loop(0, 7, to_plane, 0)
        by_plane[plane] = send[plane]
        await_bytes(by_plane.at[pl.ds(0, 7)], recv_sem.at[stage])
        mid[...] = jnp.sum(by_plane[...], axis=0)

        def to_line(index, carry):
            copy(stage + 1, mid, by_line.at[y], place(x, line_mate(index), z), gy)
            return carry

        lax.fori_loop(0, 7, to_line, 0)
        by_line[y] = mid[...]
        await_bytes(by_line.at[pl.ds(0, 7)], recv_sem.at[stage + 1])
        total[...] = jnp.sum(by_line[...], axis=0)

        def back_to_plane(index, carry):
            x_mate, z_mate = plane_mate(index)
            copy(stage + 2, total, everything.at[plane], place(x_mate, y, z_mate), gy)
            return carry

        lax.fori_loop(0, 7, back_to_plane, 0)
        everything[plane] = total[...]
        await_bytes(everything.at[pl.ds(0, 7)], recv_sem.at[stage + 2])

    loads[0].wait()
    loads[1].wait()
    hidden = hidden_in[...].astype(jnp.float32)
    squares = jnp.broadcast_to(jnp.sum(hidden * hidden, axis=1, keepdims=True), (ROWS, HD))
    gain = norm_gain[...].astype(jnp.float32).reshape(1, -1)
    scaled_in = (hidden * gain).astype(jnp.bfloat16)
    loads[2].wait()
    query_part = jnp.dot(scaled_in, w_query[...], preferred_element_type=jnp.float32)
    for j in range(SLICES):
        in_send[j, :ROWS, :] = query_part[:, j * 2 * HD : (j * 2 + 1) * HD]
        in_send[j, ROWS:PAIR, :] = query_part[:, (j * 2 + 1) * HD : (j * 2 + 2) * HD]
    loads[3].wait()
    keyval_part = jnp.dot(scaled_in, w_keyval[...], preferred_element_type=jnp.float32)
    extras = [keyval_part[:, :HD], keyval_part[:, HD:], squares, jnp.zeros((2, HD), jnp.float32)]
    slot = 0
    for extra in extras:
        for r in range(extra.shape[0]):
            in_send[slot // 4, PAIR + slot % 4 : PAIR + slot % 4 + 1, :] = extra[r : r + 1]
            slot += 1

    @pl.when(merges)
    def _():
        pl.semaphore_wait(barrier, 21 + 7)

    @pl.when(jnp.logical_not(merges))
    def _():
        pl.semaphore_wait(barrier, 21)

    all_reduce(0, in_send, in_plane, in_mid, in_line, in_sum, in_all)

    def extra_row(kind, r):
        slot = kind * ROWS + r
        return in_all[slot // 4, PAIR + slot % 4 : PAIR + slot % 4 + 1, :]

    loads[4].wait()
    score_scale = HD ** (-0.5)
    position = gx * SPAN + lax.broadcasted_iota(jnp.int32, (GROUP, SPAN), 1)
    first = gx == 0
    queries, scores, values_new, scores_new = [], [], [], []
    for r in range(ROWS):
        inv_rms = lax.rsqrt(extra_row(2, r) / D + 1e-05)
        query = jnp.concatenate([in_all[:, r, :], in_all[:, ROWS + r, :]], axis=0)
        query = (query * inv_rms).astype(jnp.bfloat16)
        key_new = (extra_row(0, r) * inv_rms).astype(jnp.bfloat16).astype(jnp.float32)
        values_new.append((extra_row(1, r) * inv_rms).astype(jnp.bfloat16).astype(jnp.float32))
        score_new = (
            jnp.sum(query.astype(jnp.float32) * key_new, axis=1, keepdims=True) * score_scale
        )
        scores_new.append(jnp.where(first, score_new, -1e30))
        scores.append(
            lax.dot_general(
                query, keys[r, 0], (((1,), (1,)), ((), ())), preferred_element_type=jnp.float32
            )
            * score_scale
        )
    loads[5].wait()
    head_row = lax.broadcasted_iota(jnp.int32, (GROUP, HD), 0)
    lane = lax.broadcasted_iota(jnp.int32, (GROUP, HD), 1) - ROWS * (head_row // SLICES)
    peaks = jnp.zeros((GROUP, HD), jnp.float32)
    totals = jnp.zeros((GROUP, HD), jnp.float32)
    for r in range(ROWS):
        valid = position < lengths_ref[r]
        masked = jnp.where(valid, scores[r], -1e30)
        peak = jnp.maximum(jnp.max(masked, axis=1, keepdims=True), scores_new[r])
        weights = jnp.where(valid, jnp.exp(masked - peak), 0.0)
        fresh = jnp.where(first, jnp.exp(scores_new[r] - peak), 0.0)
        total = jnp.sum(weights, axis=1, keepdims=True) + fresh
        accum = jnp.dot(
            weights.astype(jnp.bfloat16), values[r, 0], preferred_element_type=jnp.float32
        )
        accum = accum + fresh * values_new[r]
        soft_send[:, r, :] = accum[:SLICES]
        soft_send[:, ROWS + r, :] = accum[SLICES:]
        peaks = jnp.where(lane == r, peak, peaks)
        totals = jnp.where(lane == r, total, totals)
    soft_send[:, PEAK, :] = peaks[:SLICES] + peaks[SLICES:]
    soft_send[:, TOTAL, :] = totals[:SLICES] + totals[SLICES:]
    soft_send[:, TOTAL + 1, :] = jnp.zeros((SLICES, HD), jnp.float32)
    soft_send[:, TOTAL + 2, :] = jnp.zeros((SLICES, HD), jnp.float32)

    def to_merger(index, carry):
        y_to, z_to = (gy % 2) * 4 + index // 2, index % 2

        @pl.when((y_to != y) | (z_to != z))
        def _():
            copy(3, soft_send.at[index], soft_recv.at[y * 2 + z], place(x, y_to, z_to), gy)

        return carry

    lax.fori_loop(0, SLICES, to_merger, 0)

    @pl.when(merges)
    def _():
        soft_recv[y * 2 + z] = soft_send[(y % 4) * 2 + z]
        await_bytes(soft_recv.at[pl.ds(0, 15)], recv_sem.at[3])
        accum, peak, total, _ = merge_partials(soft_recv, 16)
        soft_mid[...] = accum
        soft_mid[PEAK : PEAK + 1, :] = peak
        soft_mid[TOTAL : TOTAL + 1, :] = total

        def to_outputs(index, carry):
            gy_to = (gy + 4 + index) % 8

            @pl.when((gy_to != gy) | (x != gy // 2))
            def _():
                copy(4, soft_mid, attn_recv.at[x], place(gy // 2, y, z), gy_to)

            return carry

        lax.fori_loop(0, 8, to_outputs, 0)

    @pl.when(source_gy == gy)
    def _():
        attn_recv[x] = soft_mid[...]
        await_bytes(attn_recv.at[pl.ds(0, 3)], recv_sem.at[4])

    @pl.when(source_gy != gy)
    def _():
        await_bytes(attn_recv, recv_sem.at[4])

    accum, _, _, columns = merge_partials(attn_recv, 4)
    attention = (accum[:PAIR] / columns[:PAIR, 4:5]).astype(jnp.bfloat16)
    attention = jnp.concatenate([attention[:ROWS], attention[ROWS:]], axis=1)
    loads[6].wait()
    out_part = jnp.dot(attention, w_output[...], preferred_element_type=jnp.float32)
    for j in range(SLICES):
        out_send[j, :ROWS, :] = out_part[:, j * 2 * HD : (j * 2 + 1) * HD]
        out_send[j, ROWS:, :] = out_part[:, (j * 2 + 1) * HD : (j * 2 + 2) * HD]
    all_reduce(5, out_send, out_plane, out_mid, out_line, out_sum, out_all)
    for j in range(SLICES):
        out_ref[:, j * 2 * HD : (j * 2 + 1) * HD] = out_all[j, :ROWS, :]
        out_ref[:, (j * 2 + 1) * HD : (j * 2 + 2) * HD] = out_all[j, ROWS:, :]

    for stage in range(3):
        await_bytes(in_all.at[pl.ds(0, 7)], send_sem.at[stage])
        await_bytes(out_all.at[pl.ds(0, 7)], send_sem.at[5 + stage])

    @pl.when(merges)
    def _():
        await_bytes(soft_recv.at[pl.ds(0, 7)], send_sem.at[3])

    @pl.when(jnp.logical_not(merges))
    def _():
        await_bytes(soft_recv.at[pl.ds(0, 8)], send_sem.at[3])

    @pl.when(merges & (x == gy // 2))
    def _():
        await_bytes(soft_recv.at[pl.ds(0, 7)], send_sem.at[4])

    @pl.when(merges & (x != gy // 2))
    def _():
        await_bytes(soft_recv.at[pl.ds(0, 8)], send_sem.at[4])


def per_device(hidden_in, norm_gain, w_query, w_keyval, w_output, key_cache, value_cache, lengths):
    hbm = pl.BlockSpec(memory_space=pl.ANY)

    def reduction(rows):
        return [
            pltpu.VMEM((SLICES, rows, HD), jnp.float32),
            pltpu.VMEM((SLICES, rows, HD), jnp.float32),
            pltpu.VMEM((rows, HD), jnp.float32),
            pltpu.VMEM((SLICES, rows, HD), jnp.float32),
            pltpu.VMEM((rows, HD), jnp.float32),
            pltpu.VMEM((SLICES, rows, HD), jnp.float32),
        ]

    scratch = [
        pltpu.VMEM(hidden_in.shape, jnp.bfloat16),
        pltpu.VMEM(norm_gain.shape, jnp.bfloat16),
        pltpu.VMEM(w_query.shape, jnp.bfloat16),
        pltpu.VMEM(w_keyval.shape, jnp.bfloat16),
        pltpu.VMEM(w_output.shape, jnp.bfloat16),
        pltpu.VMEM(key_cache.shape, jnp.bfloat16),
        pltpu.VMEM(value_cache.shape, jnp.bfloat16),
        *reduction(BLOCK),
        pltpu.VMEM((SLICES, BLOCK, HD), jnp.float32),
        pltpu.VMEM((16, BLOCK, HD), jnp.float32),
        pltpu.VMEM((BLOCK, HD), jnp.float32),
        pltpu.VMEM((4, BLOCK, HD), jnp.float32),
        *reduction(PAIR),
        pltpu.SemaphoreType.DMA((7,)),
        pltpu.SemaphoreType.DMA((8,)),
        pltpu.SemaphoreType.DMA((8,)),
    ]
    out = pl.pallas_call(
        kernel,
        out_shape=jax.ShapeDtypeStruct((ROWS, GROUP * HD), jnp.float32),
        in_specs=[hbm] * 7 + [pl.BlockSpec(memory_space=pltpu.SMEM)],
        out_specs=pl.BlockSpec(memory_space=pltpu.VMEM),
        scratch_shapes=scratch,
        compiler_params=pltpu.CompilerParams(
            collective_id=0, has_side_effects=True, vmem_limit_bytes=60 * 2**20
        ),
    )(hidden_in, norm_gain, w_query, w_keyval, w_output, key_cache, value_cache, lengths)
    return out.astype(jnp.bfloat16)


def solution(mesh):
    return jax.shard_map(
        per_device,
        mesh=mesh,
        in_specs=(
            P(None, "gx"),
            P("gx"),
            P("gx", "gy"),
            P("gx", "gy"),
            P("gx", "gy"),
            P(None, "gy", "gx", None),
            P(None, "gy", "gx", None),
            P(),
        ),
        out_specs=P(None, "gy"),
        check_vma=False,
    )
```

```python
import jax
import jax.numpy as jnp
from jax import lax
from jax.experimental import pallas as pl
from jax.experimental.pallas import tpu as pltpu
from jax.sharding import PartitionSpec as P

D = 16384
HEADS = 128
KV = 8
HD = 128
ROWS = 10
GROUP = HEADS // KV
SPAN = 512
MESH = pl.DeviceIdType.MESH

SLICES = 8
PAIR = 2 * ROWS
BLOCK = PAIR + 4
PEAK = PAIR
TOTAL = PAIR + 1


def offset(index, size):
    return size // 2 + (1 - 2 * (index % 2)) * ((index + 1) // 2)


def await_bytes(ref, sem):
    pltpu.make_async_copy(ref, ref, sem).wait()


def merge_partials(blocks, count):
    peaks = blocks[:, PEAK, :]
    peak = jnp.max(peaks, axis=0, keepdims=True)
    factors = jnp.exp(peaks - peak)
    total = jnp.sum(factors * blocks[:, TOTAL, :], axis=0, keepdims=True)
    if count < 8:
        factors = jnp.concatenate([factors, jnp.broadcast_to(total, (8 - count, HD))], axis=0)
    columns = jnp.transpose(factors)
    accum = columns[:BLOCK, 0:1] * blocks[0]
    for k in range(1, count):
        accum = accum + columns[:BLOCK, k : k + 1] * blocks[k]
    return accum, peak, total, columns


def kernel(
    hidden_hbm, gain_hbm, w_query_hbm, w_keyval_hbm, w_output_hbm, key_hbm, value_hbm, lengths_hbm,
    out_ref,
    hidden_in, norm_gain, w_query, w_keyval, w_output, keys, values, lengths,
    in_send, in_plane, in_mid, in_line, in_sum, in_all,
    soft_send, soft_recv, soft_mid, attn_recv,
    out_send, out_plane, out_mid, out_line, out_sum, out_all,
    load_sem, send_sem, recv_sem,
):
    gx, gy = lax.axis_index("gx"), lax.axis_index("gy")
    x, y, z = gx // 16, (gx // 2) % 8, gx % 2
    plane = x * 2 + z
    merges = y // 4 == gy % 2
    source_gy = 2 * x + y // 4

    def place(x, y, z):
        return x * 16 + y * 2 + z

    def plane_mate(index):
        return (x + offset(index // 2, 4)) % 4, (z + 1 - index % 2) % 2

    def line_mate(index):
        return (y + offset(index, 8)) % 8

    loads = [
        pltpu.make_async_copy(src, dst, load_sem.at[k])
        for k, (src, dst) in enumerate(
            [
                (hidden_hbm, hidden_in),
                (gain_hbm, norm_gain),
                (w_query_hbm.at[:, pl.ds(0, 1024)], w_query.at[:, pl.ds(0, 1024)]),
                (w_query_hbm.at[:, pl.ds(1024, 1024)], w_query.at[:, pl.ds(1024, 1024)]),
                (w_keyval_hbm, w_keyval),
                (key_hbm, keys),
                (value_hbm, values),
                (w_output_hbm, w_output),
                (lengths_hbm, lengths),
            ]
        )
    ]
    for load in loads[:5]:
        load.start()

    barrier = pltpu.get_barrier_semaphore()

    def signal(gx_to, gy_to):
        pl.semaphore_signal(barrier, inc=1, device_id=(gx_to, gy_to), device_id_type=MESH)

    for index in range(7):
        x_mate, z_mate = plane_mate(index)
        signal(place(x_mate, y, z_mate), gy)
    for index in range(7):
        y_mate = line_mate(index)
        signal(place(x, y_mate, 1 - z), gy)
        signal(place(x, y_mate, z), gy)

    @pl.when(source_gy != gy)
    def _():
        for index in range(4):
            signal(place(index, y, z), source_gy)

    def copy(stage, src, dst, gx_to, gy_to):
        pltpu.make_async_remote_copy(
            src_ref=src, dst_ref=dst, send_sem=send_sem.at[stage], recv_sem=recv_sem.at[stage],
            device_id=(gx_to, gy_to), device_id_type=MESH,
        ).start()

    def all_reduce(stage, send, by_plane, mid, by_line, total, everything):
        def to_plane(index, carry):
            x_mate, z_mate = plane_mate(index)
            copy(stage, send.at[x_mate * 2 + z_mate], by_plane.at[plane], place(x_mate, y, z_mate), gy)
            return carry

        lax.fori_loop(0, 7, to_plane, 0, unroll=True)
        if stage == 0:
            for load in loads[5:]:
                load.start()
        by_plane[plane] = send[plane]
        await_bytes(by_plane.at[pl.ds(0, 7)], recv_sem.at[stage])
        mid[...] = jnp.sum(by_plane[...], axis=0)

        def to_line(index, carry):
            copy(stage + 1, mid, by_line.at[y], place(x, line_mate(index), z), gy)
            return carry

        lax.fori_loop(0, 7, to_line, 0, unroll=True)
        by_line[y] = mid[...]
        await_bytes(by_line.at[pl.ds(0, 7)], recv_sem.at[stage + 1])
        total[...] = jnp.sum(by_line[...], axis=0)

        def back_to_plane(index, carry):
            x_mate, z_mate = plane_mate(index)
            copy(stage + 2, total, everything.at[plane], place(x_mate, y, z_mate), gy)
            return carry

        lax.fori_loop(0, 7, back_to_plane, 0, unroll=True)
        everything[plane] = total[...]
        await_bytes(everything.at[pl.ds(0, 7)], recv_sem.at[stage + 2])

    loads[0].wait()
    loads[1].wait()
    hidden = hidden_in[...].astype(jnp.float32)
    squares = jnp.broadcast_to(jnp.sum(hidden * hidden, axis=1, keepdims=True), (ROWS, HD))
    gain = norm_gain[...].astype(jnp.float32).reshape(1, -1)
    scaled_in = (hidden * gain).astype(jnp.bfloat16)
    for part in range(2):
        loads[2 + part].wait()
        columns = slice(part * 1024, (part + 1) * 1024)
        query_part = jnp.dot(scaled_in, w_query[:, columns], preferred_element_type=jnp.float32)
        for k in range(4):
            j = part * 4 + k
            in_send[j, :ROWS, :] = query_part[:, k * 2 * HD : (k * 2 + 1) * HD]
            in_send[j, ROWS:PAIR, :] = query_part[:, (k * 2 + 1) * HD : (k * 2 + 2) * HD]
    loads[4].wait()
    keyval_part = jnp.dot(scaled_in, w_keyval[...], preferred_element_type=jnp.float32)
    extras = [keyval_part[:, :HD], keyval_part[:, HD:], squares, jnp.zeros((2, HD), jnp.float32)]
    slot = 0
    for extra in extras:
        for r in range(extra.shape[0]):
            in_send[slot // 4, PAIR + slot % 4 : PAIR + slot % 4 + 1, :] = extra[r : r + 1]
            slot += 1

    @pl.when(merges)
    def _():
        pl.semaphore_wait(barrier, 21 + 7)

    @pl.when(jnp.logical_not(merges))
    def _():
        pl.semaphore_wait(barrier, 21)

    all_reduce(0, in_send, in_plane, in_mid, in_line, in_sum, in_all)

    def extra_row(kind, r):
        slot = kind * ROWS + r
        return in_all[slot // 4, PAIR + slot % 4 : PAIR + slot % 4 + 1, :]

    loads[5].wait()
    loads[8].wait()
    score_scale = HD ** (-0.5)
    position = gx * SPAN + lax.broadcasted_iota(jnp.int32, (GROUP, SPAN), 1)
    first = gx == 0
    queries, scores, values_new, scores_new = [], [], [], []
    for r in range(ROWS):
        inv_rms = lax.rsqrt(extra_row(2, r) / D + 1e-05)
        query = jnp.concatenate([in_all[:, r, :], in_all[:, ROWS + r, :]], axis=0)
        query = (query * inv_rms).astype(jnp.bfloat16)
        key_new = (extra_row(0, r) * inv_rms).astype(jnp.bfloat16).astype(jnp.float32)
        values_new.append((extra_row(1, r) * inv_rms).astype(jnp.bfloat16).astype(jnp.float32))
        score_new = (
            jnp.sum(query.astype(jnp.float32) * key_new, axis=1, keepdims=True) * score_scale
        )
        scores_new.append(jnp.where(first, score_new, -1e30))
        scores.append(
            lax.dot_general(
                query, keys[r, 0], (((1,), (1,)), ((), ())), preferred_element_type=jnp.float32
            )
            * score_scale
        )
    loads[6].wait()
    head_row = lax.broadcasted_iota(jnp.int32, (GROUP, HD), 0)
    lane = lax.broadcasted_iota(jnp.int32, (GROUP, HD), 1) - ROWS * (head_row // SLICES)
    peaks = jnp.zeros((GROUP, HD), jnp.float32)
    totals = jnp.zeros((GROUP, HD), jnp.float32)
    for r in range(ROWS):
        valid = position < lengths[r]
        masked = jnp.where(valid, scores[r], -1e30)
        peak = jnp.maximum(jnp.max(masked, axis=1, keepdims=True), scores_new[r])
        weights = jnp.where(valid, jnp.exp(masked - peak), 0.0)
        fresh = jnp.where(first, jnp.exp(scores_new[r] - peak), 0.0)
        total = jnp.sum(weights, axis=1, keepdims=True) + fresh
        accum = jnp.dot(
            weights.astype(jnp.bfloat16), values[r, 0], preferred_element_type=jnp.float32
        )
        accum = accum + fresh * values_new[r]
        soft_send[:, r, :] = accum[:SLICES]
        soft_send[:, ROWS + r, :] = accum[SLICES:]
        peaks = jnp.where(lane == r, peak, peaks)
        totals = jnp.where(lane == r, total, totals)
    soft_send[:, PEAK, :] = peaks[:SLICES] + peaks[SLICES:]
    soft_send[:, TOTAL, :] = totals[:SLICES] + totals[SLICES:]
    soft_send[:, TOTAL + 1, :] = jnp.zeros((SLICES, HD), jnp.float32)
    soft_send[:, TOTAL + 2, :] = jnp.zeros((SLICES, HD), jnp.float32)

    def to_merger(index, carry):
        y_to, z_to = (gy % 2) * 4 + index // 2, index % 2

        @pl.when((y_to != y) | (z_to != z))
        def _():
            copy(3, soft_send.at[index], soft_recv.at[y * 2 + z], place(x, y_to, z_to), gy)

        return carry

    lax.fori_loop(0, SLICES, to_merger, 0)

    @pl.when(merges)
    def _():
        soft_recv[y * 2 + z] = soft_send[(y % 4) * 2 + z]
        await_bytes(soft_recv.at[pl.ds(0, 15)], recv_sem.at[3])
        accum, peak, total, _ = merge_partials(soft_recv, 16)
        soft_mid[...] = accum
        soft_mid[PEAK : PEAK + 1, :] = peak
        soft_mid[TOTAL : TOTAL + 1, :] = total

        def to_outputs(index, carry):
            gy_to = (gy + 4 + index) % 8

            @pl.when((gy_to != gy) | (x != gy // 2))
            def _():
                copy(4, soft_mid, attn_recv.at[x], place(gy // 2, y, z), gy_to)

            return carry

        lax.fori_loop(0, 8, to_outputs, 0)

    @pl.when(source_gy == gy)
    def _():
        attn_recv[x] = soft_mid[...]
        await_bytes(attn_recv.at[pl.ds(0, 3)], recv_sem.at[4])

    @pl.when(source_gy != gy)
    def _():
        await_bytes(attn_recv, recv_sem.at[4])

    accum, _, _, columns = merge_partials(attn_recv, 4)
    attention = (accum[:PAIR] / columns[:PAIR, 4:5]).astype(jnp.bfloat16)
    attention = jnp.concatenate([attention[:ROWS], attention[ROWS:]], axis=1)
    loads[7].wait()
    out_part = jnp.dot(attention, w_output[...], preferred_element_type=jnp.float32)
    for j in range(SLICES):
        out_send[j, :ROWS, :] = out_part[:, j * 2 * HD : (j * 2 + 1) * HD]
        out_send[j, ROWS:, :] = out_part[:, (j * 2 + 1) * HD : (j * 2 + 2) * HD]
    all_reduce(5, out_send, out_plane, out_mid, out_line, out_sum, out_all)
    for j in range(SLICES):
        out_ref[:, j * 2 * HD : (j * 2 + 1) * HD] = out_all[j, :ROWS, :]
        out_ref[:, (j * 2 + 1) * HD : (j * 2 + 2) * HD] = out_all[j, ROWS:, :]

    for stage in range(3):
        await_bytes(in_all.at[pl.ds(0, 7)], send_sem.at[stage])
        await_bytes(out_all.at[pl.ds(0, 7)], send_sem.at[5 + stage])

    @pl.when(merges)
    def _():
        await_bytes(soft_recv.at[pl.ds(0, 7)], send_sem.at[3])

    @pl.when(jnp.logical_not(merges))
    def _():
        await_bytes(soft_recv.at[pl.ds(0, 8)], send_sem.at[3])

    @pl.when(merges & (x == gy // 2))
    def _():
        await_bytes(soft_recv.at[pl.ds(0, 7)], send_sem.at[4])

    @pl.when(merges & (x != gy // 2))
    def _():
        await_bytes(soft_recv.at[pl.ds(0, 8)], send_sem.at[4])


def per_device(hidden_in, norm_gain, w_query, w_keyval, w_output, key_cache, value_cache, lengths):
    hbm = pl.BlockSpec(memory_space=pltpu.HBM)

    def reduction(rows):
        return [
            pltpu.VMEM((SLICES, rows, HD), jnp.float32),
            pltpu.VMEM((SLICES, rows, HD), jnp.float32),
            pltpu.VMEM((rows, HD), jnp.float32),
            pltpu.VMEM((SLICES, rows, HD), jnp.float32),
            pltpu.VMEM((rows, HD), jnp.float32),
            pltpu.VMEM((SLICES, rows, HD), jnp.float32),
        ]

    scratch = [
        pltpu.VMEM(hidden_in.shape, jnp.bfloat16),
        pltpu.VMEM(norm_gain.shape, jnp.bfloat16),
        pltpu.VMEM(w_query.shape, jnp.bfloat16),
        pltpu.VMEM(w_keyval.shape, jnp.bfloat16),
        pltpu.VMEM(w_output.shape, jnp.bfloat16),
        pltpu.VMEM(key_cache.shape, jnp.bfloat16),
        pltpu.VMEM(value_cache.shape, jnp.bfloat16),
        pltpu.SMEM(lengths.shape, jnp.int32),
        *reduction(BLOCK),
        pltpu.VMEM((SLICES, BLOCK, HD), jnp.float32),
        pltpu.VMEM((16, BLOCK, HD), jnp.float32),
        pltpu.VMEM((BLOCK, HD), jnp.float32),
        pltpu.VMEM((4, BLOCK, HD), jnp.float32),
        *reduction(PAIR),
        pltpu.SemaphoreType.DMA((9,)),
        pltpu.SemaphoreType.DMA((8,)),
        pltpu.SemaphoreType.DMA((8,)),
    ]
    out = pl.pallas_call(
        kernel,
        out_shape=jax.ShapeDtypeStruct((ROWS, GROUP * HD), jnp.float32),
        in_specs=[hbm] * 8,
        out_specs=pl.BlockSpec(memory_space=pltpu.VMEM),
        scratch_shapes=scratch,
        compiler_params=pltpu.CompilerParams(
            collective_id=0, has_side_effects=True, vmem_limit_bytes=16 * 2**20
        ),
    )(*[pltpu.with_memory_space_constraint(a, pltpu.HBM) for a in (hidden_in, norm_gain, w_query, w_keyval, w_output, key_cache, value_cache, lengths)])
    return out.astype(jnp.bfloat16)


def solution(mesh):
    return jax.shard_map(
        per_device,
        mesh=mesh,
        in_specs=(
            P(None, "gx"),
            P("gx"),
            P("gx", "gy"),
            P("gx", "gy"),
            P("gx", "gy"),
            P(None, "gy", "gx", None),
            P(None, "gy", "gx", None),
            P(),
        ),
        out_specs=P(None, "gy"),
        check_vma=False,
    )
```

```python
import jax
import jax.numpy as jnp
from jax import lax
from jax.experimental import pallas as pl
from jax.experimental.pallas import tpu as pltpu
from jax.sharding import PartitionSpec as P

D = 16384
HEADS = 128
KV = 8
HD = 128
ROWS = 10
GROUP = HEADS // KV
SPAN = 512
MESH = pl.DeviceIdType.MESH

SLICES = 8
PAIR = 2 * ROWS
BLOCK = PAIR + 4
SOFT = 32
PEAK = PAIR
TOTAL = PEAK + 3


def offset(index, size):
    return size // 2 + (1 - 2 * (index % 2)) * ((index + 1) // 2)


def await_bytes(ref, sem):
    pltpu.make_async_copy(ref, ref, sem).wait()


def split(value):
    high = value.astype(jnp.bfloat16).astype(jnp.float32)
    rest = value - high
    middle = rest.astype(jnp.bfloat16).astype(jnp.float32)
    return high, middle, rest - middle


def merge_partials(blocks, count):
    def joined(row):
        return blocks[:count, row, :] + blocks[:count, row + 1, :] + blocks[:count, row + 2, :]

    peaks = joined(PEAK)
    peak = jnp.max(peaks, axis=0, keepdims=True)
    factors = jnp.exp(peaks - peak)
    total = jnp.sum(factors * joined(TOTAL), axis=0, keepdims=True)
    if count < 8:
        factors = jnp.concatenate([factors, jnp.broadcast_to(total, (8 - count, HD))], axis=0)
    columns = jnp.transpose(factors)
    accum = columns[:BLOCK, 0:1] * blocks[0, :BLOCK]
    for k in range(1, count):
        accum = accum + columns[:BLOCK, k : k + 1] * blocks[k, :BLOCK]
    return accum, peak, total, columns


def kernel(
    hidden_hbm, gain_hbm, w_query_hbm, w_keyval_hbm, w_output_hbm, key_hbm, value_hbm, lengths_hbm,
    out_ref,
    hidden_in, norm_gain, w_query, w_keyval, w_output, keys, values, lengths, keys_across,
    in_send, in_plane, in_mid, in_line, in_sum, in_all,
    soft_wide, soft_send, soft_recv, soft_mid, attn_recv,
    out_send, out_plane, out_mid, out_line, out_sum, out_all,
    load_sem, send_sem, recv_sem,
):
    gx, gy = lax.axis_index("gx"), lax.axis_index("gy")
    x, y, z = gx // 16, (gx // 2) % 8, gx % 2
    plane = x * 2 + z
    merges = y // 4 == gy % 2
    source_gy = 2 * x + y // 4

    def place(x, y, z):
        return x * 16 + y * 2 + z

    def plane_mate(index):
        return (x + offset(index // 2, 4)) % 4, (z + 1 - index % 2) % 2

    def line_mate(index):
        return (y + offset(index, 8)) % 8

    loads = [
        pltpu.make_async_copy(src, dst, load_sem.at[k])
        for k, (src, dst) in enumerate(
            [
                (hidden_hbm, hidden_in),
                (gain_hbm, norm_gain),
                (w_query_hbm.at[:, pl.ds(0, 1024)], w_query.at[:, pl.ds(0, 1024)]),
                (w_query_hbm.at[:, pl.ds(1024, 1024)], w_query.at[:, pl.ds(1024, 1024)]),
                (w_keyval_hbm, w_keyval),
                (key_hbm, keys),
                (value_hbm, values),
                (w_output_hbm, w_output),
                (lengths_hbm, lengths),
            ]
        )
    ]

    barrier = pltpu.get_barrier_semaphore()

    def signal(gx_to, gy_to):
        pl.semaphore_signal(barrier, inc=1, device_id=(gx_to, gy_to), device_id_type=MESH)

    @pl.when(source_gy != gy)
    def _():
        for index in range(4):
            signal(place(index, y, z), source_gy)

    for index in range(7):
        x_mate, z_mate = plane_mate(index)
        signal(place(x_mate, y, z_mate), gy)
    for index in range(7):
        y_mate = line_mate(index)
        signal(place(x, y_mate, z), gy)

    for load in loads[:5]:
        load.start()

    def copy(stage, src, dst, gx_to, gy_to):
        pltpu.make_async_remote_copy(
            src_ref=src, dst_ref=dst, send_sem=send_sem.at[stage], recv_sem=recv_sem.at[stage],
            device_id=(gx_to, gy_to), device_id_type=MESH,
        ).start()

    def all_reduce(stage, send, by_plane, mid, by_line, total, everything):
        def to_plane(index, carry):
            x_mate, z_mate = plane_mate(index)
            copy(stage, send.at[x_mate * 2 + z_mate], by_plane.at[plane], place(x_mate, y, z_mate), gy)
            return carry

        lax.fori_loop(0, 7, to_plane, 0, unroll=True)
        if stage == 0:
            for load in loads[5:]:
                load.start()
        by_plane[plane] = send[plane]
        await_bytes(by_plane.at[pl.ds(0, 7)], recv_sem.at[stage])
        mid[...] = jnp.sum(by_plane[...], axis=0)

        def to_line(index, carry):
            copy(stage + 1, mid, by_line.at[y], place(x, line_mate(index), z), gy)
            return carry

        lax.fori_loop(0, 7, to_line, 0, unroll=True)
        if stage == 0:
            loads[5].wait()
            for r in range(ROWS):
                keys_across[r] = jnp.transpose(keys[r, 0])
        by_line[y] = mid[...]
        await_bytes(by_line.at[pl.ds(0, 7)], recv_sem.at[stage + 1])
        total[...] = jnp.sum(by_line[...], axis=0)

        def back_to_plane(index, carry):
            x_mate, z_mate = plane_mate(index)
            copy(stage + 2, total, everything.at[plane], place(x_mate, y, z_mate), gy)
            return carry

        lax.fori_loop(0, 7, back_to_plane, 0, unroll=True)
        everything[plane] = total[...]
        await_bytes(everything.at[pl.ds(0, 7)], recv_sem.at[stage + 2])

    loads[0].wait()
    loads[1].wait()
    hidden = hidden_in[...].astype(jnp.float32)
    squares = jnp.broadcast_to(jnp.sum(hidden * hidden, axis=1, keepdims=True), (ROWS, HD))
    gain = norm_gain[...].astype(jnp.float32).reshape(1, -1)
    scaled_in = (hidden * gain).astype(jnp.bfloat16)
    for part in range(2):
        loads[2 + part].wait()
        columns = slice(part * 1024, (part + 1) * 1024)
        query_part = jnp.dot(scaled_in, w_query[:, columns], preferred_element_type=jnp.float32)
        for k in range(4):
            j = part * 4 + k
            in_send[j, :ROWS, :] = query_part[:, k * 2 * HD : (k * 2 + 1) * HD]
            in_send[j, ROWS:PAIR, :] = query_part[:, (k * 2 + 1) * HD : (k * 2 + 2) * HD]
    loads[4].wait()
    keyval_part = jnp.dot(scaled_in, w_keyval[...], preferred_element_type=jnp.float32)
    extras = [keyval_part[:, :HD], keyval_part[:, HD:], squares, jnp.zeros((2, HD), jnp.float32)]
    slot = 0
    for extra in extras:
        for r in range(extra.shape[0]):
            in_send[slot // 4, PAIR + slot % 4 : PAIR + slot % 4 + 1, :] = extra[r : r + 1]
            slot += 1

    @pl.when(merges)
    def _():
        pl.semaphore_wait(barrier, 14 + 7)

    @pl.when(jnp.logical_not(merges))
    def _():
        pl.semaphore_wait(barrier, 14)

    all_reduce(0, in_send, in_plane, in_mid, in_line, in_sum, in_all)

    def extra_row(kind, r):
        slot = kind * ROWS + r
        return in_all[slot // 4, PAIR + slot % 4 : PAIR + slot % 4 + 1, :]

    loads[8].wait()
    score_scale = HD ** (-0.5)
    position = gx * SPAN + lax.broadcasted_iota(jnp.int32, (GROUP, SPAN), 1)
    first = gx == 0
    queries, scores, values_new, scores_new = [], [], [], []
    for r in range(ROWS):
        inv_rms = lax.rsqrt(extra_row(2, r) / D + 1e-05)
        query = jnp.concatenate([in_all[:, r, :], in_all[:, ROWS + r, :]], axis=0)
        query = (query * inv_rms).astype(jnp.bfloat16)
        key_new = (extra_row(0, r) * inv_rms).astype(jnp.bfloat16).astype(jnp.float32)
        values_new.append((extra_row(1, r) * inv_rms).astype(jnp.bfloat16).astype(jnp.float32))
        score_new = (
            jnp.sum(query.astype(jnp.float32) * key_new, axis=1, keepdims=True) * score_scale
        )
        scores_new.append(jnp.where(first, score_new, -1e30))
        scores.append(
            jnp.dot(query, keys_across[r], preferred_element_type=jnp.float32)
            * score_scale
        )
    loads[6].wait()
    head_row = lax.broadcasted_iota(jnp.int32, (GROUP, HD), 0)
    lane = lax.broadcasted_iota(jnp.int32, (GROUP, HD), 1) - ROWS * (head_row // SLICES)
    peaks = jnp.zeros((GROUP, HD), jnp.float32)
    totals = jnp.zeros((GROUP, HD), jnp.float32)
    for r in range(ROWS):
        valid = position < lengths[r]
        masked = jnp.where(valid, scores[r], -1e30)
        peak = jnp.maximum(jnp.max(masked, axis=1, keepdims=True), scores_new[r])
        weights = jnp.where(valid, jnp.exp(masked - peak), 0.0)
        fresh = jnp.where(first, jnp.exp(scores_new[r] - peak), 0.0)
        total = jnp.sum(weights, axis=1, keepdims=True) + fresh
        accum = jnp.dot(
            weights.astype(jnp.bfloat16), values[r, 0], preferred_element_type=jnp.float32
        )
        accum = accum + fresh * values_new[r]
        soft_wide[:SLICES, r, :] = accum[:SLICES]
        soft_wide[:SLICES, ROWS + r, :] = accum[SLICES:]
        peaks = jnp.where(lane == r, peak, peaks)
        totals = jnp.where(lane == r, total, totals)
    terms = split(peaks[:SLICES] + peaks[SLICES:]) + split(totals[:SLICES] + totals[SLICES:])
    for k in range(SOFT - PEAK):
        term = terms[k] if k < 6 else jnp.zeros((SLICES, HD), jnp.float32)
        soft_wide[:SLICES, PEAK + k, :] = term
    soft_send[...] = soft_wide[:SLICES].astype(jnp.bfloat16)

    def to_merger(index, carry):
        y_to, z_to = (gy % 2) * 4 + index // 2, index % 2

        @pl.when((y_to != y) | (z_to != z))
        def _():
            copy(3, soft_send.at[index], soft_recv.at[y * 2 + z], place(x, y_to, z_to), gy)

        return carry

    lax.fori_loop(0, SLICES, to_merger, 0)

    @pl.when(merges)
    def _():
        soft_recv[y * 2 + z] = soft_send[(y % 4) * 2 + z]
        await_bytes(soft_recv.at[pl.ds(0, 15)], recv_sem.at[3])
        soft_wide[...] = soft_recv[...].astype(jnp.float32)
        accum, peak, total, _ = merge_partials(soft_wide, 16)
        merged = soft_wide.at[0]
        merged[:BLOCK, :] = accum
        merged[BLOCK:, :] = jnp.zeros((SOFT - BLOCK, HD), jnp.float32)
        for k, term in enumerate(split(peak) + split(total)):
            merged[PEAK + k : PEAK + k + 1, :] = term
        soft_mid[...] = merged[...].astype(jnp.bfloat16)

        def to_outputs(index, carry):
            gy_to = index

            @pl.when((gy_to != gy) | (x != gy // 2))
            def _():
                copy(4, soft_mid, attn_recv.at[x], place(gy // 2, y, z), gy_to)

            return carry

        lax.fori_loop(0, 8, to_outputs, 0)

    @pl.when(source_gy == gy)
    def _():
        attn_recv[x] = soft_mid[...]
        await_bytes(attn_recv.at[pl.ds(0, 3)], recv_sem.at[4])

    @pl.when(source_gy != gy)
    def _():
        await_bytes(attn_recv, recv_sem.at[4])

    soft_wide[:4] = attn_recv[...].astype(jnp.float32)
    accum, _, _, columns = merge_partials(soft_wide, 4)
    attention = (accum[:PAIR] / columns[:PAIR, 4:5]).astype(jnp.bfloat16)
    attention = jnp.concatenate([attention[:ROWS], attention[ROWS:]], axis=1)
    loads[7].wait()
    out_part = jnp.dot(attention, w_output[...], preferred_element_type=jnp.float32)
    for j in range(SLICES):
        out_send[j, :ROWS, :] = out_part[:, j * 2 * HD : (j * 2 + 1) * HD]
        out_send[j, ROWS:, :] = out_part[:, (j * 2 + 1) * HD : (j * 2 + 2) * HD]
    all_reduce(5, out_send, out_plane, out_mid, out_line, out_sum, out_all)
    for j in range(SLICES):
        out_ref[:, j * 2 * HD : (j * 2 + 1) * HD] = out_all[j, :ROWS, :]
        out_ref[:, (j * 2 + 1) * HD : (j * 2 + 2) * HD] = out_all[j, ROWS:, :]

    for stage in range(3):
        await_bytes(in_all.at[pl.ds(0, 7)], send_sem.at[stage])
        await_bytes(out_all.at[pl.ds(0, 7)], send_sem.at[5 + stage])

    @pl.when(merges)
    def _():
        await_bytes(soft_recv.at[pl.ds(0, 7)], send_sem.at[3])

    @pl.when(jnp.logical_not(merges))
    def _():
        await_bytes(soft_recv.at[pl.ds(0, 8)], send_sem.at[3])

    @pl.when(merges & (x == gy // 2))
    def _():
        await_bytes(soft_recv.at[pl.ds(0, 7)], send_sem.at[4])

    @pl.when(merges & (x != gy // 2))
    def _():
        await_bytes(soft_recv.at[pl.ds(0, 8)], send_sem.at[4])


def per_device(hidden_in, norm_gain, w_query, w_keyval, w_output, key_cache, value_cache, lengths):
    hbm = pl.BlockSpec(memory_space=pltpu.HBM)

    def reduction(rows):
        return [
            pltpu.VMEM((SLICES, rows, HD), jnp.float32),
            pltpu.VMEM((SLICES, rows, HD), jnp.float32),
            pltpu.VMEM((rows, HD), jnp.float32),
            pltpu.VMEM((SLICES, rows, HD), jnp.float32),
            pltpu.VMEM((rows, HD), jnp.float32),
            pltpu.VMEM((SLICES, rows, HD), jnp.float32),
        ]

    scratch = [
        pltpu.VMEM(hidden_in.shape, jnp.bfloat16),
        pltpu.VMEM(norm_gain.shape, jnp.bfloat16),
        pltpu.VMEM(w_query.shape, jnp.bfloat16),
        pltpu.VMEM(w_keyval.shape, jnp.bfloat16),
        pltpu.VMEM(w_output.shape, jnp.bfloat16),
        pltpu.VMEM(key_cache.shape, jnp.bfloat16),
        pltpu.VMEM(value_cache.shape, jnp.bfloat16),
        pltpu.SMEM(lengths.shape, jnp.int32),
        pltpu.VMEM((ROWS, HD, SPAN), jnp.bfloat16),
        *reduction(BLOCK),
        pltpu.VMEM((16, SOFT, HD), jnp.float32),
        pltpu.VMEM((SLICES, SOFT, HD), jnp.bfloat16),
        pltpu.VMEM((16, SOFT, HD), jnp.bfloat16),
        pltpu.VMEM((SOFT, HD), jnp.bfloat16),
        pltpu.VMEM((4, SOFT, HD), jnp.bfloat16),
        *reduction(PAIR),
        pltpu.SemaphoreType.DMA((9,)),
        pltpu.SemaphoreType.DMA((8,)),
        pltpu.SemaphoreType.DMA((8,)),
    ]
    out = pl.pallas_call(
        kernel,
        out_shape=jax.ShapeDtypeStruct((ROWS, GROUP * HD), jnp.float32),
        in_specs=[hbm] * 8,
        out_specs=pl.BlockSpec(memory_space=pltpu.VMEM),
        scratch_shapes=scratch,
        compiler_params=pltpu.CompilerParams(
            collective_id=0, has_side_effects=True, vmem_limit_bytes=16 * 2**20
        ),
    )(*[pltpu.with_memory_space_constraint(a, pltpu.HBM) for a in (hidden_in, norm_gain, w_query, w_keyval, w_output, key_cache, value_cache, lengths)])
    return out.astype(jnp.bfloat16)


def solution(mesh):
    return jax.shard_map(
        per_device,
        mesh=mesh,
        in_specs=(
            P(None, "gx"),
            P("gx"),
            P("gx", "gy"),
            P("gx", "gy"),
            P("gx", "gy"),
            P(None, "gy", "gx", None),
            P(None, "gy", "gx", None),
            P(),
        ),
        out_specs=P(None, "gy"),
        check_vma=False,
    )
```

```python
import jax
import jax.numpy as jnp
from jax import lax
from jax.experimental import pallas as pl
from jax.experimental.pallas import tpu as pltpu
from jax.sharding import PartitionSpec as P

D = 16384
HEADS = 128
KV = 8
HD = 128
ROWS = 10
GROUP = HEADS // KV
SPAN = 512
MESH = pl.DeviceIdType.MESH

SLICES = 8
PAIR = 2 * ROWS
BLOCK = PAIR + 4
SOFT = 32
PEAK = PAIR
TOTAL = PEAK + 3


def offset(index, size):
    return size // 2 + (1 - 2 * (index % 2)) * ((index + 1) // 2)


def await_bytes(ref, sem):
    pltpu.make_async_copy(ref, ref, sem).wait()


def split(value):
    high = value.astype(jnp.bfloat16).astype(jnp.float32)
    rest = value - high
    middle = rest.astype(jnp.bfloat16).astype(jnp.float32)
    return high, middle, rest - middle


def merge_partials(blocks, count):
    def joined(row):
        return blocks[:count, row, :] + blocks[:count, row + 1, :] + blocks[:count, row + 2, :]

    peaks = joined(PEAK)
    peak = jnp.max(peaks, axis=0, keepdims=True)
    factors = jnp.exp(peaks - peak)
    total = jnp.sum(factors * joined(TOTAL), axis=0, keepdims=True)
    if count < 8:
        factors = jnp.concatenate([factors, jnp.broadcast_to(total, (8 - count, HD))], axis=0)
    columns = jnp.transpose(factors)
    accum = columns[:BLOCK, 0:1] * blocks[0, :BLOCK]
    for k in range(1, count):
        accum = accum + columns[:BLOCK, k : k + 1] * blocks[k, :BLOCK]
    return accum, peak, total, columns


def kernel(
    hidden_hbm, gain_hbm, w_query_hbm, w_keyval_hbm, w_output_hbm, key_hbm, value_hbm, lengths_hbm,
    out_ref,
    hidden_in, norm_gain, w_query, w_keyval, w_output, keys, values, lengths, keys_across,
    in_send, in_plane, in_mid, in_line, in_sum, in_all,
    soft_wide, soft_send, soft_recv, soft_mid, attn_recv,
    out_send, out_plane, out_mid, out_line, out_sum, out_all,
    load_sem, send_sem, recv_sem, late_sem,
):
    gx, gy = lax.axis_index("gx"), lax.axis_index("gy")
    x, y, z = gx // 16, (gx // 2) % 8, gx % 2
    plane = x * 2 + z
    merges = y // 4 == gy % 2
    source_gy = 2 * x + y // 4

    def is_late(y):
        return (y + 5) % 8 < 4

    def place(x, y, z):
        return x * 16 + y * 2 + z

    def plane_mate(index):
        return (x + offset(index // 2, 4)) % 4, (z + 1 - index % 2) % 2

    def line_mate(index):
        return (y + offset(index, 8)) % 8

    loads = [
        pltpu.make_async_copy(src, dst, load_sem.at[k])
        for k, (src, dst) in enumerate(
            [
                (hidden_hbm, hidden_in),
                (gain_hbm, norm_gain),
                (w_query_hbm.at[:, pl.ds(0, 1024)], w_query.at[:, pl.ds(0, 1024)]),
                (w_query_hbm.at[:, pl.ds(1024, 1024)], w_query.at[:, pl.ds(1024, 1024)]),
                (w_keyval_hbm, w_keyval),
                (key_hbm, keys),
                (value_hbm, values),
                (w_output_hbm, w_output),
                (lengths_hbm, lengths),
            ]
        )
    ]

    barrier = pltpu.get_barrier_semaphore()

    def signal(gx_to, gy_to):
        pl.semaphore_signal(barrier, inc=1, device_id=(gx_to, gy_to), device_id_type=MESH)

    @pl.when(source_gy != gy)
    def _():
        signal(gx, source_gy)

    for index in range(7):
        x_mate, z_mate = plane_mate(index)
        signal(place(x_mate, y, z_mate), gy)
    for index in range(7):
        y_mate = line_mate(index)

        @pl.when(is_late(y_mate) | jnp.logical_not(is_late(y)))
        def _():
            signal(place(x, y_mate, z), gy)

    for load in loads[:5]:
        load.start()

    def copy(stage, src, dst, gx_to, gy_to):
        pltpu.make_async_remote_copy(
            src_ref=src, dst_ref=dst, send_sem=send_sem.at[stage], recv_sem=recv_sem.at[stage],
            device_id=(gx_to, gy_to), device_id_type=MESH,
        ).start()

    def all_reduce(stage, send, by_plane, mid, by_line, total, everything):
        def to_plane(index, carry):
            x_mate, z_mate = plane_mate(index)
            copy(stage, send.at[x_mate * 2 + z_mate], by_plane.at[plane], place(x_mate, y, z_mate), gy)
            return carry

        lax.fori_loop(0, 7, to_plane, 0, unroll=True)
        if stage == 0:
            for load in loads[5:]:
                load.start()
        by_plane[plane] = send[plane]
        await_bytes(by_plane.at[pl.ds(0, 7)], recv_sem.at[stage])
        mid[...] = jnp.sum(by_plane[...], axis=0)
        if stage == 0:

            @pl.when(jnp.logical_not(is_late(y)))
            def _():
                pl.semaphore_wait(late_sem, 4)

        def to_line(index, carry):
            copy(stage + 1, mid, by_line.at[y], place(x, line_mate(index), z), gy)
            return carry

        lax.fori_loop(0, 7, to_line, 0, unroll=True)
        if stage == 0:
            loads[5].wait()
            for r in range(ROWS):
                keys_across[r] = jnp.transpose(keys[r, 0])
        by_line[y] = mid[...]
        await_bytes(by_line.at[pl.ds(0, 7)], recv_sem.at[stage + 1])
        total[...] = jnp.sum(by_line[...], axis=0)

        def back_to_plane(index, carry):
            x_mate, z_mate = plane_mate(index)
            copy(stage + 2, total, everything.at[plane], place(x_mate, y, z_mate), gy)
            return carry

        lax.fori_loop(0, 7, back_to_plane, 0, unroll=True)
        everything[plane] = total[...]
        await_bytes(everything.at[pl.ds(0, 7)], recv_sem.at[stage + 2])

    loads[0].wait()
    loads[1].wait()
    hidden = hidden_in[...].astype(jnp.float32)
    squares = jnp.broadcast_to(jnp.sum(hidden * hidden, axis=1, keepdims=True), (ROWS, HD))
    gain = norm_gain[...].astype(jnp.float32).reshape(1, -1)
    scaled_in = (hidden * gain).astype(jnp.bfloat16)
    for part in range(2):
        loads[2 + part].wait()
        columns = slice(part * 1024, (part + 1) * 1024)
        query_part = jnp.dot(scaled_in, w_query[:, columns], preferred_element_type=jnp.float32)
        for k in range(4):
            j = part * 4 + k
            in_send[j, :ROWS, :] = query_part[:, k * 2 * HD : (k * 2 + 1) * HD]
            in_send[j, ROWS:PAIR, :] = query_part[:, (k * 2 + 1) * HD : (k * 2 + 2) * HD]
    loads[4].wait()
    keyval_part = jnp.dot(scaled_in, w_keyval[...], preferred_element_type=jnp.float32)
    extras = [keyval_part[:, :HD], keyval_part[:, HD:], squares, jnp.zeros((2, HD), jnp.float32)]
    slot = 0
    for extra in extras:
        for r in range(extra.shape[0]):
            in_send[slot // 4, PAIR + slot % 4 : PAIR + slot % 4 + 1, :] = extra[r : r + 1]
            slot += 1

    greetings = 10 + 4 * is_late(y).astype(jnp.int32) + 7 * (source_gy == gy).astype(jnp.int32)
    pl.semaphore_wait(barrier, greetings)

    @pl.when(is_late(y))
    def _():
        for y_mate in (0, 1, 7, 2):
            pl.semaphore_signal(
                late_sem, inc=1, device_id=(place(x, y_mate, z), gy), device_id_type=MESH
            )

    all_reduce(0, in_send, in_plane, in_mid, in_line, in_sum, in_all)

    def extra_row(kind, r):
        slot = kind * ROWS + r
        return in_all[slot // 4, PAIR + slot % 4 : PAIR + slot % 4 + 1, :]

    loads[8].wait()
    score_scale = HD ** (-0.5)
    position = gx * SPAN + lax.broadcasted_iota(jnp.int32, (GROUP, SPAN), 1)
    first = gx == 0
    queries, scores, values_new, scores_new = [], [], [], []
    for r in range(ROWS):
        inv_rms = lax.rsqrt(extra_row(2, r) / D + 1e-05)
        query = jnp.concatenate([in_all[:, r, :], in_all[:, ROWS + r, :]], axis=0)
        query = (query * inv_rms).astype(jnp.bfloat16)
        key_new = (extra_row(0, r) * inv_rms).astype(jnp.bfloat16).astype(jnp.float32)
        values_new.append((extra_row(1, r) * inv_rms).astype(jnp.bfloat16).astype(jnp.float32))
        score_new = (
            jnp.sum(query.astype(jnp.float32) * key_new, axis=1, keepdims=True) * score_scale
        )
        scores_new.append(jnp.where(first, score_new, -1e30))
        scores.append(
            jnp.dot(query, keys_across[r], preferred_element_type=jnp.float32)
            * score_scale
        )
    loads[6].wait()
    head_row = lax.broadcasted_iota(jnp.int32, (GROUP, HD), 0)
    lane = lax.broadcasted_iota(jnp.int32, (GROUP, HD), 1) - ROWS * (head_row // SLICES)
    peaks = jnp.zeros((GROUP, HD), jnp.float32)
    totals = jnp.zeros((GROUP, HD), jnp.float32)
    for r in range(ROWS):
        valid = position < lengths[r]
        masked = jnp.where(valid, scores[r], -1e30)
        peak = jnp.maximum(jnp.max(masked, axis=1, keepdims=True), scores_new[r])
        weights = jnp.where(valid, jnp.exp(masked - peak), 0.0)
        fresh = jnp.where(first, jnp.exp(scores_new[r] - peak), 0.0)
        total = jnp.sum(weights, axis=1, keepdims=True) + fresh
        accum = jnp.dot(
            weights.astype(jnp.bfloat16), values[r, 0], preferred_element_type=jnp.float32
        )
        accum = accum + fresh * values_new[r]
        soft_wide[:SLICES, r, :] = accum[:SLICES]
        soft_wide[:SLICES, ROWS + r, :] = accum[SLICES:]
        peaks = jnp.where(lane == r, peak, peaks)
        totals = jnp.where(lane == r, total, totals)
    terms = split(peaks[:SLICES] + peaks[SLICES:]) + split(totals[:SLICES] + totals[SLICES:])
    for k in range(SOFT - PEAK):
        term = terms[k] if k < 6 else jnp.zeros((SLICES, HD), jnp.float32)
        soft_wide[:SLICES, PEAK + k, :] = term
    soft_send[...] = soft_wide[:SLICES].astype(jnp.bfloat16)

    def to_merger(index, carry):
        y_to, z_to = (gy % 2) * 4 + index // 2, index % 2

        @pl.when((y_to != y) | (z_to != z))
        def _():
            copy(3, soft_send.at[index], soft_recv.at[y * 2 + z], place(x, y_to, z_to), gy)

        return carry

    lax.fori_loop(0, SLICES, to_merger, 0)

    @pl.when(merges)
    def _():
        soft_recv[y * 2 + z] = soft_send[(y % 4) * 2 + z]
        await_bytes(soft_recv.at[pl.ds(0, 15)], recv_sem.at[3])
        soft_wide[...] = soft_recv[...].astype(jnp.float32)
        accum, peak, total, _ = merge_partials(soft_wide, 16)
        merged = soft_wide.at[0]
        merged[:BLOCK, :] = accum
        merged[BLOCK:, :] = jnp.zeros((SOFT - BLOCK, HD), jnp.float32)
        for k, term in enumerate(split(peak) + split(total)):
            merged[PEAK + k : PEAK + k + 1, :] = term
        soft_mid[...] = merged[...].astype(jnp.bfloat16)

        def to_outputs(index, carry):
            gy_to = index

            @pl.when((gy_to != gy) | (x != gy // 2))
            def _():
                copy(4, soft_mid, attn_recv.at[x], place(gy // 2, y, z), gy_to)

            return carry

        lax.fori_loop(0, 8, to_outputs, 0)

    @pl.when(source_gy == gy)
    def _():
        attn_recv[x] = soft_mid[...]
        await_bytes(attn_recv.at[pl.ds(0, 3)], recv_sem.at[4])

    @pl.when(source_gy != gy)
    def _():
        await_bytes(attn_recv, recv_sem.at[4])

    soft_wide[:4] = attn_recv[...].astype(jnp.float32)
    accum, _, _, columns = merge_partials(soft_wide, 4)
    attention = (accum[:PAIR] / columns[:PAIR, 4:5]).astype(jnp.bfloat16)
    attention = jnp.concatenate([attention[:ROWS], attention[ROWS:]], axis=1)
    loads[7].wait()
    out_part = jnp.dot(attention, w_output[...], preferred_element_type=jnp.float32)
    for j in range(SLICES):
        out_send[j, :ROWS, :] = out_part[:, j * 2 * HD : (j * 2 + 1) * HD]
        out_send[j, ROWS:, :] = out_part[:, (j * 2 + 1) * HD : (j * 2 + 2) * HD]
    all_reduce(5, out_send, out_plane, out_mid, out_line, out_sum, out_all)
    for j in range(SLICES):
        out_ref[:, j * 2 * HD : (j * 2 + 1) * HD] = out_all[j, :ROWS, :]
        out_ref[:, (j * 2 + 1) * HD : (j * 2 + 2) * HD] = out_all[j, ROWS:, :]

    for stage in range(3):
        await_bytes(in_all.at[pl.ds(0, 7)], send_sem.at[stage])
        await_bytes(out_all.at[pl.ds(0, 7)], send_sem.at[5 + stage])

    @pl.when(merges)
    def _():
        await_bytes(soft_recv.at[pl.ds(0, 7)], send_sem.at[3])

    @pl.when(jnp.logical_not(merges))
    def _():
        await_bytes(soft_recv.at[pl.ds(0, 8)], send_sem.at[3])

    @pl.when(merges & (x == gy // 2))
    def _():
        await_bytes(soft_recv.at[pl.ds(0, 7)], send_sem.at[4])

    @pl.when(merges & (x != gy // 2))
    def _():
        await_bytes(soft_recv.at[pl.ds(0, 8)], send_sem.at[4])


def per_device(hidden_in, norm_gain, w_query, w_keyval, w_output, key_cache, value_cache, lengths):
    hbm = pl.BlockSpec(memory_space=pltpu.HBM)

    def reduction(rows):
        return [
            pltpu.VMEM((SLICES, rows, HD), jnp.float32),
            pltpu.VMEM((SLICES, rows, HD), jnp.float32),
            pltpu.VMEM((rows, HD), jnp.float32),
            pltpu.VMEM((SLICES, rows, HD), jnp.float32),
            pltpu.VMEM((rows, HD), jnp.float32),
            pltpu.VMEM((SLICES, rows, HD), jnp.float32),
        ]

    scratch = [
        pltpu.VMEM(hidden_in.shape, jnp.bfloat16),
        pltpu.VMEM(norm_gain.shape, jnp.bfloat16),
        pltpu.VMEM(w_query.shape, jnp.bfloat16),
        pltpu.VMEM(w_keyval.shape, jnp.bfloat16),
        pltpu.VMEM(w_output.shape, jnp.bfloat16),
        pltpu.VMEM(key_cache.shape, jnp.bfloat16),
        pltpu.VMEM(value_cache.shape, jnp.bfloat16),
        pltpu.SMEM(lengths.shape, jnp.int32),
        pltpu.VMEM((ROWS, HD, SPAN), jnp.bfloat16),
        *reduction(BLOCK),
        pltpu.VMEM((16, SOFT, HD), jnp.float32),
        pltpu.VMEM((SLICES, SOFT, HD), jnp.bfloat16),
        pltpu.VMEM((16, SOFT, HD), jnp.bfloat16),
        pltpu.VMEM((SOFT, HD), jnp.bfloat16),
        pltpu.VMEM((4, SOFT, HD), jnp.bfloat16),
        *reduction(PAIR),
        pltpu.SemaphoreType.DMA((9,)),
        pltpu.SemaphoreType.DMA((8,)),
        pltpu.SemaphoreType.DMA((8,)),
        pltpu.SemaphoreType.REGULAR,
    ]
    out = pl.pallas_call(
        kernel,
        out_shape=jax.ShapeDtypeStruct((ROWS, GROUP * HD), jnp.float32),
        in_specs=[hbm] * 8,
        out_specs=pl.BlockSpec(memory_space=pltpu.VMEM),
        scratch_shapes=scratch,
        compiler_params=pltpu.CompilerParams(
            collective_id=0, has_side_effects=True, vmem_limit_bytes=16 * 2**20
        ),
    )(*[pltpu.with_memory_space_constraint(a, pltpu.HBM) for a in (hidden_in, norm_gain, w_query, w_keyval, w_output, key_cache, value_cache, lengths)])
    return out.astype(jnp.bfloat16)


def solution(mesh):
    return jax.shard_map(
        per_device,
        mesh=mesh,
        in_specs=(
            P(None, "gx"),
            P("gx"),
            P("gx", "gy"),
            P("gx", "gy"),
            P("gx", "gy"),
            P(None, "gy", "gx", None),
            P(None, "gy", "gx", None),
            P(),
        ),
        out_specs=P(None, "gy"),
        check_vma=False,
    )
```

```python
import jax
import jax.numpy as jnp
from jax import lax
from jax.experimental import pallas as pl
from jax.experimental.pallas import tpu as pltpu
from jax.sharding import PartitionSpec as P

D = 16384
HEADS = 128
KV = 8
HD = 128
ROWS = 10
GROUP = HEADS // KV
SPAN = 512
MESH = pl.DeviceIdType.MESH

SLICES = 8
PAIR = 2 * ROWS
BLOCK = PAIR + 4
SOFT = 32
PEAK = PAIR
TOTAL = PEAK + 3


def offset(index, size):
    return size // 2 + (1 - 2 * (index % 2)) * ((index + 1) // 2)


def await_bytes(ref, sem):
    pltpu.make_async_copy(ref, ref, sem).wait()


def split(value):
    high = value.astype(jnp.bfloat16).astype(jnp.float32)
    rest = value - high
    middle = rest.astype(jnp.bfloat16).astype(jnp.float32)
    return high, middle, rest - middle


def merge_partials(blocks, count):
    def joined(row):
        return blocks[:count, row, :] + blocks[:count, row + 1, :] + blocks[:count, row + 2, :]

    peaks = joined(PEAK)
    peak = jnp.max(peaks, axis=0, keepdims=True)
    factors = jnp.exp(peaks - peak)
    total = jnp.sum(factors * joined(TOTAL), axis=0, keepdims=True)
    if count < 8:
        factors = jnp.concatenate([factors, jnp.broadcast_to(total, (8 - count, HD))], axis=0)
    columns = jnp.transpose(factors)
    accum = columns[:BLOCK, 0:1] * blocks[0, :BLOCK]
    for k in range(1, count):
        accum = accum + columns[:BLOCK, k : k + 1] * blocks[k, :BLOCK]
    return accum, peak, total, columns


def kernel(
    hidden_hbm, gain_hbm, w_query_hbm, w_keyval_hbm, w_output_hbm, key_hbm, value_hbm, lengths_hbm,
    out_ref,
    hidden_in, norm_gain, w_query, w_keyval, w_output, keys, values, lengths, keys_across,
    in_send, in_plane, in_mid, in_line, in_sum, in_all,
    soft_wide, soft_send, soft_recv, soft_mid, attn_recv,
    out_send, out_plane, out_mid, out_line, out_sum, out_all,
    load_sem, send_sem, recv_sem, late_sem,
):
    gx, gy = lax.axis_index("gx"), lax.axis_index("gy")
    x, y, z = gx // 16, (gx // 2) % 8, gx % 2
    plane = x * 2 + z
    merges = y // 4 == gy % 2
    source_gy = 2 * x + y // 4

    def is_late(y):
        return (y + 5) % 8 < 4

    def place(x, y, z):
        return x * 16 + y * 2 + z

    def plane_mate(index):
        return (x + offset(index // 2, 4)) % 4, (z + 1 - index % 2) % 2

    def line_mate(index):
        return (y + offset(index, 8)) % 8

    loads = [
        pltpu.make_async_copy(src, dst, load_sem.at[k])
        for k, (src, dst) in enumerate(
            [
                (hidden_hbm, hidden_in),
                (gain_hbm, norm_gain),
                (w_query_hbm.at[:, pl.ds(0, 1024)], w_query.at[:, pl.ds(0, 1024)]),
                (w_query_hbm.at[:, pl.ds(1024, 1024)], w_query.at[:, pl.ds(1024, 1024)]),
                (w_keyval_hbm, w_keyval),
                (key_hbm, keys),
                (value_hbm, values),
                (w_output_hbm, w_output),
                (lengths_hbm, lengths),
            ]
        )
    ]

    barrier = pltpu.get_barrier_semaphore()

    def signal(gx_to, gy_to):
        pl.semaphore_signal(barrier, inc=1, device_id=(gx_to, gy_to), device_id_type=MESH)

    @pl.when(source_gy != gy)
    def _():
        signal(gx, source_gy)

    for index in range(7):
        x_mate, z_mate = plane_mate(index)
        signal(place(x_mate, y, z_mate), gy)
    for index in range(7):
        y_mate = line_mate(index)

        @pl.when(is_late(y_mate) | jnp.logical_not(is_late(y)))
        def _():
            signal(place(x, y_mate, z), gy)

    for load in loads[:5]:
        load.start()

    def copy(stage, src, dst, gx_to, gy_to):
        pltpu.make_async_remote_copy(
            src_ref=src, dst_ref=dst, send_sem=send_sem.at[stage], recv_sem=recv_sem.at[stage],
            device_id=(gx_to, gy_to), device_id_type=MESH,
        ).start()

    def all_reduce(stage, send, by_plane, mid, by_line, total, everything):
        def to_plane(index, carry):
            x_mate, z_mate = plane_mate(index)
            copy(stage, send.at[x_mate * 2 + z_mate], by_plane.at[plane], place(x_mate, y, z_mate), gy)
            return carry

        lax.fori_loop(0, 7, to_plane, 0, unroll=True)
        if stage == 0:
            for load in loads[5:]:
                load.start()
        by_plane[plane] = send[plane]
        await_bytes(by_plane.at[pl.ds(0, 7)], recv_sem.at[stage])
        mid[...] = jnp.sum(by_plane[...], axis=0)
        if stage == 0:

            @pl.when(jnp.logical_not(is_late(y)))
            def _():
                pl.semaphore_wait(late_sem, 4)

        def to_line(index, carry):
            copy(stage + 1, mid, by_line.at[y], place(x, line_mate(index), z), gy)
            return carry

        lax.fori_loop(0, 7, to_line, 0, unroll=True)
        if stage == 0:
            loads[5].wait()
            for r in range(ROWS):
                keys_across[r] = jnp.transpose(keys[r, 0])
        by_line[y] = mid[...]
        await_bytes(by_line.at[pl.ds(0, 7)], recv_sem.at[stage + 1])
        total[...] = jnp.sum(by_line[...], axis=0)

        def back_to_plane(index, carry):
            x_mate, z_mate = plane_mate(index)
            copy(stage + 2, total, everything.at[plane], place(x_mate, y, z_mate), gy)
            return carry

        lax.fori_loop(0, 7, back_to_plane, 0, unroll=True)
        everything[plane] = total[...]
        await_bytes(everything.at[pl.ds(0, 7)], recv_sem.at[stage + 2])

    loads[0].wait()
    loads[1].wait()
    hidden = hidden_in[...].astype(jnp.float32)
    squares = jnp.broadcast_to(jnp.sum(hidden * hidden, axis=1, keepdims=True), (ROWS, HD))
    gain = norm_gain[...].astype(jnp.float32).reshape(1, -1)
    scaled_in = (hidden * gain).astype(jnp.bfloat16)
    for part in range(2):
        loads[2 + part].wait()
        columns = slice(part * 1024, (part + 1) * 1024)
        query_part = jnp.dot(scaled_in, w_query[:, columns], preferred_element_type=jnp.float32)
        for k in range(4):
            j = part * 4 + k
            in_send[j, :ROWS, :] = query_part[:, k * 2 * HD : (k * 2 + 1) * HD]
            in_send[j, ROWS:PAIR, :] = query_part[:, (k * 2 + 1) * HD : (k * 2 + 2) * HD]
    loads[4].wait()
    keyval_part = jnp.dot(scaled_in, w_keyval[...], preferred_element_type=jnp.float32)
    extras = [keyval_part[:, :HD], keyval_part[:, HD:], squares, jnp.zeros((2, HD), jnp.float32)]
    slot = 0
    for extra in extras:
        for r in range(extra.shape[0]):
            in_send[slot // 4, PAIR + slot % 4 : PAIR + slot % 4 + 1, :] = extra[r : r + 1]
            slot += 1

    greetings = 10 + 4 * is_late(y).astype(jnp.int32) + 7 * (source_gy == gy).astype(jnp.int32)
    pl.semaphore_wait(barrier, greetings)

    @pl.when(is_late(y))
    def _():
        for y_mate in (0, 1, 7, 2):
            pl.semaphore_signal(
                late_sem, inc=1, device_id=(place(x, y_mate, z), gy), device_id_type=MESH
            )

    all_reduce(0, in_send, in_plane, in_mid, in_line, in_sum, in_all)

    def extra_row(kind, r):
        slot = kind * ROWS + r
        return in_all[slot // 4, PAIR + slot % 4 : PAIR + slot % 4 + 1, :]

    loads[8].wait()
    score_scale = HD ** (-0.5)
    position = gx * SPAN + lax.broadcasted_iota(jnp.int32, (GROUP, SPAN), 1)
    first = gx == 0
    queries, scores, values_new, scores_new = [], [], [], []
    for r in range(ROWS):
        inv_rms = lax.rsqrt(extra_row(2, r) / D + 1e-05)
        query = jnp.concatenate([in_all[:, r, :], in_all[:, ROWS + r, :]], axis=0)
        query = (query * inv_rms).astype(jnp.bfloat16)
        key_new = (extra_row(0, r) * inv_rms).astype(jnp.bfloat16).astype(jnp.float32)
        values_new.append((extra_row(1, r) * inv_rms).astype(jnp.bfloat16).astype(jnp.float32))
        score_new = (
            jnp.sum(query.astype(jnp.float32) * key_new, axis=1, keepdims=True) * score_scale
        )
        scores_new.append(jnp.where(first, score_new, -1e30))
        scores.append(
            jnp.dot(query, keys_across[r], preferred_element_type=jnp.float32)
            * score_scale
        )
    loads[6].wait()
    head_row = lax.broadcasted_iota(jnp.int32, (GROUP, HD), 0)
    lane = lax.broadcasted_iota(jnp.int32, (GROUP, HD), 1) - ROWS * (head_row // SLICES)
    peaks = jnp.zeros((GROUP, HD), jnp.float32)
    totals = jnp.zeros((GROUP, HD), jnp.float32)
    for r in range(ROWS):
        valid = position < lengths[r]
        masked = jnp.where(valid, scores[r], -1e30)
        peak = jnp.maximum(jnp.max(masked, axis=1, keepdims=True), scores_new[r])
        peak = jnp.maximum(peak, -1e29)
        weights = jnp.exp(masked - peak)
        fresh = jnp.where(first, jnp.exp(scores_new[r] - peak), 0.0)
        total = jnp.sum(weights, axis=1, keepdims=True) + fresh
        accum = jnp.dot(
            weights.astype(jnp.bfloat16), values[r, 0], preferred_element_type=jnp.float32
        )
        accum = accum + fresh * values_new[r]
        soft_wide[:SLICES, r, :] = accum[:SLICES]
        soft_wide[:SLICES, ROWS + r, :] = accum[SLICES:]
        peaks = jnp.where(lane == r, peak, peaks)
        totals = jnp.where(lane == r, total, totals)
    terms = split(peaks[:SLICES] + peaks[SLICES:]) + split(totals[:SLICES] + totals[SLICES:])
    for k in range(SOFT - PEAK):
        term = terms[k] if k < 6 else jnp.zeros((SLICES, HD), jnp.float32)
        soft_wide[:SLICES, PEAK + k, :] = term
    soft_send[...] = soft_wide[:SLICES].astype(jnp.bfloat16)

    for index in range(8):
        y_to = (y + offset(index, 8)) % 8
        for z_step in (1, 0):
            if index == 7 and z_step == 0:
                continue
            z_to = (z + z_step) % 2

            @pl.when(y_to // 4 == gy % 2)
            def _():
                copy(3, soft_send.at[(y_to % 4) * 2 + z_to], soft_recv.at[y * 2 + z], place(x, y_to, z_to), gy)

    @pl.when(merges)
    def _():
        soft_recv[y * 2 + z] = soft_send[(y % 4) * 2 + z]
        await_bytes(soft_recv.at[pl.ds(0, 15)], recv_sem.at[3])
        soft_wide[...] = soft_recv[...].astype(jnp.float32)
        accum, peak, total, _ = merge_partials(soft_wide, 16)
        merged = soft_wide.at[0]
        merged[:BLOCK, :] = accum
        merged[BLOCK:, :] = jnp.zeros((SOFT - BLOCK, HD), jnp.float32)
        for k, term in enumerate(split(peak) + split(total)):
            merged[PEAK + k : PEAK + k + 1, :] = term
        soft_mid[...] = merged[...].astype(jnp.bfloat16)

        def to_outputs(index, carry):
            gy_to = index

            @pl.when((gy_to != gy) | (x != gy // 2))
            def _():
                copy(4, soft_mid, attn_recv.at[x], place(gy // 2, y, z), gy_to)

            return carry

        lax.fori_loop(0, 8, to_outputs, 0, unroll=True)

    @pl.when(source_gy == gy)
    def _():
        attn_recv[x] = soft_mid[...]
        await_bytes(attn_recv.at[pl.ds(0, 3)], recv_sem.at[4])

    @pl.when(source_gy != gy)
    def _():
        await_bytes(attn_recv, recv_sem.at[4])

    soft_wide[:4] = attn_recv[...].astype(jnp.float32)
    accum, _, _, columns = merge_partials(soft_wide, 4)
    attention = (accum[:PAIR] / columns[:PAIR, 4:5]).astype(jnp.bfloat16)
    attention = jnp.concatenate([attention[:ROWS], attention[ROWS:]], axis=1)
    loads[7].wait()
    out_part = jnp.dot(attention, w_output[...], preferred_element_type=jnp.float32)
    for j in range(SLICES):
        out_send[j, :ROWS, :] = out_part[:, j * 2 * HD : (j * 2 + 1) * HD]
        out_send[j, ROWS:, :] = out_part[:, (j * 2 + 1) * HD : (j * 2 + 2) * HD]
    all_reduce(5, out_send, out_plane, out_mid, out_line, out_sum, out_all)
    for j in range(SLICES):
        out_ref[:, j * 2 * HD : (j * 2 + 1) * HD] = out_all[j, :ROWS, :]
        out_ref[:, (j * 2 + 1) * HD : (j * 2 + 2) * HD] = out_all[j, ROWS:, :]

    for stage in range(3):
        await_bytes(in_all.at[pl.ds(0, 7)], send_sem.at[stage])
        await_bytes(out_all.at[pl.ds(0, 7)], send_sem.at[5 + stage])

    @pl.when(merges)
    def _():
        await_bytes(soft_recv.at[pl.ds(0, 7)], send_sem.at[3])

    @pl.when(jnp.logical_not(merges))
    def _():
        await_bytes(soft_recv.at[pl.ds(0, 8)], send_sem.at[3])

    @pl.when(merges & (x == gy // 2))
    def _():
        await_bytes(soft_recv.at[pl.ds(0, 7)], send_sem.at[4])

    @pl.when(merges & (x != gy // 2))
    def _():
        await_bytes(soft_recv.at[pl.ds(0, 8)], send_sem.at[4])


def per_device(hidden_in, norm_gain, w_query, w_keyval, w_output, key_cache, value_cache, lengths):
    hbm = pl.BlockSpec(memory_space=pltpu.HBM)

    def reduction(rows):
        return [
            pltpu.VMEM((SLICES, rows, HD), jnp.float32),
            pltpu.VMEM((SLICES, rows, HD), jnp.float32),
            pltpu.VMEM((rows, HD), jnp.float32),
            pltpu.VMEM((SLICES, rows, HD), jnp.float32),
            pltpu.VMEM((rows, HD), jnp.float32),
            pltpu.VMEM((SLICES, rows, HD), jnp.float32),
        ]

    scratch = [
        pltpu.VMEM(hidden_in.shape, jnp.bfloat16),
        pltpu.VMEM(norm_gain.shape, jnp.bfloat16),
        pltpu.VMEM(w_query.shape, jnp.bfloat16),
        pltpu.VMEM(w_keyval.shape, jnp.bfloat16),
        pltpu.VMEM(w_output.shape, jnp.bfloat16),
        pltpu.VMEM(key_cache.shape, jnp.bfloat16),
        pltpu.VMEM(value_cache.shape, jnp.bfloat16),
        pltpu.SMEM(lengths.shape, jnp.int32),
        pltpu.VMEM((ROWS, HD, SPAN), jnp.bfloat16),
        *reduction(BLOCK),
        pltpu.VMEM((16, SOFT, HD), jnp.float32),
        pltpu.VMEM((SLICES, SOFT, HD), jnp.bfloat16),
        pltpu.VMEM((16, SOFT, HD), jnp.bfloat16),
        pltpu.VMEM((SOFT, HD), jnp.bfloat16),
        pltpu.VMEM((4, SOFT, HD), jnp.bfloat16),
        *reduction(PAIR),
        pltpu.SemaphoreType.DMA((9,)),
        pltpu.SemaphoreType.DMA((8,)),
        pltpu.SemaphoreType.DMA((8,)),
        pltpu.SemaphoreType.REGULAR,
    ]
    out = pl.pallas_call(
        kernel,
        out_shape=jax.ShapeDtypeStruct((ROWS, GROUP * HD), jnp.float32),
        in_specs=[hbm] * 8,
        out_specs=pl.BlockSpec(memory_space=pltpu.VMEM),
        scratch_shapes=scratch,
        compiler_params=pltpu.CompilerParams(
            collective_id=0, has_side_effects=True, vmem_limit_bytes=16 * 2**20
        ),
    )(*[pltpu.with_memory_space_constraint(a, pltpu.HBM) for a in (hidden_in, norm_gain, w_query, w_keyval, w_output, key_cache, value_cache, lengths)])
    return out.astype(jnp.bfloat16)


def solution(mesh):
    return jax.shard_map(
        per_device,
        mesh=mesh,
        in_specs=(
            P(None, "gx"),
            P("gx"),
            P("gx", "gy"),
            P("gx", "gy"),
            P("gx", "gy"),
            P(None, "gy", "gx", None),
            P(None, "gy", "gx", None),
            P(),
        ),
        out_specs=P(None, "gy"),
        check_vma=False,
    )
```

```python
import jax
import jax.numpy as jnp
from jax import lax
from jax.experimental import pallas as pl
from jax.experimental.pallas import tpu as pltpu
from jax.sharding import PartitionSpec as P

D = 16384
HEADS = 128
KV = 8
HD = 128
ROWS = 10
GROUP = HEADS // KV
SPAN = 512
MESH = pl.DeviceIdType.MESH

SLICES = 8
PAIR = 2 * ROWS
BLOCK = PAIR + 4
SOFT = 32
PEAK = PAIR
TOTAL = PEAK + 3


def offset(index, size):
    return size // 2 + (1 - 2 * (index % 2)) * ((index + 1) // 2)


def await_bytes(ref, sem):
    pltpu.make_async_copy(ref, ref, sem).wait()


def split(value):
    high = value.astype(jnp.bfloat16).astype(jnp.float32)
    rest = value - high
    middle = rest.astype(jnp.bfloat16).astype(jnp.float32)
    return high, middle, rest - middle


def merge_partials(blocks, count):
    def joined(row):
        return blocks[:count, row, :] + blocks[:count, row + 1, :] + blocks[:count, row + 2, :]

    peaks = joined(PEAK)
    peak = jnp.max(peaks, axis=0, keepdims=True)
    factors = jnp.exp(peaks - peak)
    total = jnp.sum(factors * joined(TOTAL), axis=0, keepdims=True)
    if count < 8:
        factors = jnp.concatenate([factors, jnp.broadcast_to(total, (8 - count, HD))], axis=0)
    columns = jnp.transpose(factors)
    accum = columns[:BLOCK, 0:1] * blocks[0, :BLOCK]
    for k in range(1, count):
        accum = accum + columns[:BLOCK, k : k + 1] * blocks[k, :BLOCK]
    return accum, peak, total, columns


def kernel(
    hidden_hbm, gain_hbm, w_query_hbm, w_keyval_hbm, w_output_hbm, key_hbm, value_hbm, lengths_hbm,
    out_ref,
    hidden_in, norm_gain, w_query, w_keyval, w_output, keys, values, lengths, keys_across,
    in_send, in_plane, in_mid, in_line, in_sum, in_all,
    soft_wide, soft_send, soft_recv, soft_mid, attn_recv,
    out_send, out_plane, out_mid, out_line, out_sum, out_all,
    load_sem, send_sem, recv_sem, late_sem,
):
    gx, gy = lax.axis_index("gx"), lax.axis_index("gy")
    x, y, z = gx // 16, (gx // 2) % 8, gx % 2
    plane = x * 2 + z
    merges = y // 4 == gy % 2
    source_gy = 2 * x + y // 4

    def is_late(y):
        return (y + 5) % 8 < 4

    def place(x, y, z):
        return x * 16 + y * 2 + z

    def plane_mate(index):
        return (x + offset(index // 2, 4)) % 4, (z + 1 - index % 2) % 2

    def line_mate(index):
        return (y + offset(index, 8)) % 8

    loads = [
        pltpu.make_async_copy(src, dst, load_sem.at[k])
        for k, (src, dst) in enumerate(
            [
                (hidden_hbm, hidden_in),
                (gain_hbm, norm_gain),
                (w_query_hbm.at[:, pl.ds(0, 1024)], w_query.at[:, pl.ds(0, 1024)]),
                (w_query_hbm.at[:, pl.ds(1024, 1024)], w_query.at[:, pl.ds(1024, 1024)]),
                (w_keyval_hbm, w_keyval),
                (key_hbm, keys),
                (value_hbm, values),
                (w_output_hbm, w_output),
                (lengths_hbm, lengths),
            ]
        )
    ]

    barrier = pltpu.get_barrier_semaphore()

    def signal(gx_to, gy_to):
        pl.semaphore_signal(barrier, inc=1, device_id=(gx_to, gy_to), device_id_type=MESH)

    @pl.when(source_gy != gy)
    def _():
        signal(gx, source_gy)

    for index in range(7):
        x_mate, z_mate = plane_mate(index)
        signal(place(x_mate, y, z_mate), gy)
    for index in range(7):
        y_mate = line_mate(index)

        @pl.when(is_late(y_mate) | jnp.logical_not(is_late(y)))
        def _():
            signal(place(x, y_mate, z), gy)

    for load in loads[:5]:
        load.start()

    def copy(stage, src, dst, gx_to, gy_to):
        pltpu.make_async_remote_copy(
            src_ref=src, dst_ref=dst, send_sem=send_sem.at[stage], recv_sem=recv_sem.at[stage],
            device_id=(gx_to, gy_to), device_id_type=MESH,
        ).start()

    def all_reduce(stage, send, by_plane, mid, by_line, total, everything):
        if stage == 0:

            def to_plane(index, carry):
                x_mate, z_mate = plane_mate(index)
                copy(stage, send.at[x_mate * 2 + z_mate], by_plane.at[plane], place(x_mate, y, z_mate), gy)
                return carry

            lax.fori_loop(0, 7, to_plane, 0, unroll=True)
        if stage == 0:
            for load in loads[5:]:
                load.start()
        by_plane[plane] = send[plane]
        await_bytes(by_plane.at[pl.ds(0, 7)], recv_sem.at[stage])
        mid[...] = jnp.sum(by_plane[...], axis=0)
        if stage == 0:

            @pl.when(jnp.logical_not(is_late(y)))
            def _():
                pl.semaphore_wait(late_sem, 4)

        def to_line(index, carry):
            copy(stage + 1, mid, by_line.at[y], place(x, line_mate(index), z), gy)
            return carry

        lax.fori_loop(0, 7, to_line, 0, unroll=True)
        if stage == 0:
            loads[5].wait()
            for r in range(ROWS):
                keys_across[r] = jnp.transpose(keys[r, 0])
        by_line[y] = mid[...]
        await_bytes(by_line.at[pl.ds(0, 7)], recv_sem.at[stage + 1])
        total[...] = jnp.sum(by_line[...], axis=0)

        def back_to_plane(index, carry):
            x_mate, z_mate = plane_mate(index)
            copy(stage + 2, total, everything.at[plane], place(x_mate, y, z_mate), gy)
            return carry

        lax.fori_loop(0, 7, back_to_plane, 0, unroll=True)
        everything[plane] = total[...]
        await_bytes(everything.at[pl.ds(0, 7)], recv_sem.at[stage + 2])

    loads[0].wait()
    loads[1].wait()
    hidden = hidden_in[...].astype(jnp.float32)
    squares = jnp.broadcast_to(jnp.sum(hidden * hidden, axis=1, keepdims=True), (ROWS, HD))
    gain = norm_gain[...].astype(jnp.float32).reshape(1, -1)
    scaled_in = (hidden * gain).astype(jnp.bfloat16)
    for part in range(2):
        loads[2 + part].wait()
        columns = slice(part * 1024, (part + 1) * 1024)
        query_part = jnp.dot(scaled_in, w_query[:, columns], preferred_element_type=jnp.float32)
        for k in range(4):
            j = part * 4 + k
            in_send[j, :ROWS, :] = query_part[:, k * 2 * HD : (k * 2 + 1) * HD]
            in_send[j, ROWS:PAIR, :] = query_part[:, (k * 2 + 1) * HD : (k * 2 + 2) * HD]
    loads[4].wait()
    keyval_part = jnp.dot(scaled_in, w_keyval[...], preferred_element_type=jnp.float32)
    extras = [keyval_part[:, :HD], keyval_part[:, HD:], squares, jnp.zeros((2, HD), jnp.float32)]
    slot = 0
    for extra in extras:
        for r in range(extra.shape[0]):
            in_send[slot // 4, PAIR + slot % 4 : PAIR + slot % 4 + 1, :] = extra[r : r + 1]
            slot += 1

    greetings = 10 + 4 * is_late(y).astype(jnp.int32) + 7 * (source_gy == gy).astype(jnp.int32)
    pl.semaphore_wait(barrier, greetings)

    @pl.when(is_late(y))
    def _():
        for y_mate in (0, 1, 7, 2):
            pl.semaphore_signal(
                late_sem, inc=1, device_id=(place(x, y_mate, z), gy), device_id_type=MESH
            )

    all_reduce(0, in_send, in_plane, in_mid, in_line, in_sum, in_all)

    def extra_row(kind, r):
        slot = kind * ROWS + r
        return in_all[slot // 4, PAIR + slot % 4 : PAIR + slot % 4 + 1, :]

    loads[8].wait()
    score_scale = HD ** (-0.5)
    position = gx * SPAN + lax.broadcasted_iota(jnp.int32, (GROUP, SPAN), 1)
    first = gx == 0
    queries, scores, values_new, scores_new = [], [], [], []
    for r in range(ROWS):
        inv_rms = lax.rsqrt(extra_row(2, r) / D + 1e-05)
        query = jnp.concatenate([in_all[:, r, :], in_all[:, ROWS + r, :]], axis=0)
        query = (query * inv_rms).astype(jnp.bfloat16)
        key_new = (extra_row(0, r) * inv_rms).astype(jnp.bfloat16).astype(jnp.float32)
        values_new.append((extra_row(1, r) * inv_rms).astype(jnp.bfloat16).astype(jnp.float32))
        score_new = (
            jnp.sum(query.astype(jnp.float32) * key_new, axis=1, keepdims=True) * score_scale
        )
        scores_new.append(jnp.where(first, score_new, -1e30))
        scores.append(
            jnp.dot(query, keys_across[r], preferred_element_type=jnp.float32)
            * score_scale
        )
    loads[6].wait()
    head_row = lax.broadcasted_iota(jnp.int32, (GROUP, HD), 0)
    lane = lax.broadcasted_iota(jnp.int32, (GROUP, HD), 1) - ROWS * (head_row // SLICES)
    peaks = jnp.zeros((GROUP, HD), jnp.float32)
    totals = jnp.zeros((GROUP, HD), jnp.float32)
    for r in range(ROWS):
        valid = position < lengths[r]
        masked = jnp.where(valid, scores[r], -1e30)
        peak = jnp.maximum(jnp.max(masked, axis=1, keepdims=True), scores_new[r])
        peak = jnp.maximum(peak, -1e29)
        weights = jnp.exp(masked - peak)
        fresh = jnp.where(first, jnp.exp(scores_new[r] - peak), 0.0)
        total = jnp.sum(weights, axis=1, keepdims=True) + fresh
        accum = jnp.dot(
            weights.astype(jnp.bfloat16), values[r, 0], preferred_element_type=jnp.float32
        )
        accum = accum + fresh * values_new[r]
        soft_wide[:SLICES, r, :] = accum[:SLICES]
        soft_wide[:SLICES, ROWS + r, :] = accum[SLICES:]
        peaks = jnp.where(lane == r, peak, peaks)
        totals = jnp.where(lane == r, total, totals)
    terms = split(peaks[:SLICES] + peaks[SLICES:]) + split(totals[:SLICES] + totals[SLICES:])
    for k in range(SOFT - PEAK):
        term = terms[k] if k < 6 else jnp.zeros((SLICES, HD), jnp.float32)
        soft_wide[:SLICES, PEAK + k, :] = term
    soft_send[...] = soft_wide[:SLICES].astype(jnp.bfloat16)

    for index in range(8):
        y_to = (y + offset(index, 8)) % 8
        for z_step in (1, 0):
            if index == 7 and z_step == 0:
                continue
            z_to = (z + z_step) % 2

            @pl.when(y_to // 4 == gy % 2)
            def _():
                copy(3, soft_send.at[(y_to % 4) * 2 + z_to], soft_recv.at[y * 2 + z], place(x, y_to, z_to), gy)

    @pl.when(merges)
    def _():
        soft_recv[y * 2 + z] = soft_send[(y % 4) * 2 + z]
        await_bytes(soft_recv.at[pl.ds(0, 15)], recv_sem.at[3])
        soft_wide[...] = soft_recv[...].astype(jnp.float32)
        accum, peak, total, _ = merge_partials(soft_wide, 16)
        merged = soft_wide.at[0]
        merged[:BLOCK, :] = accum
        merged[BLOCK:, :] = jnp.zeros((SOFT - BLOCK, HD), jnp.float32)
        for k, term in enumerate(split(peak) + split(total)):
            merged[PEAK + k : PEAK + k + 1, :] = term
        soft_mid[...] = merged[...].astype(jnp.bfloat16)

        def to_outputs(index, carry):
            gy_to = index

            @pl.when((gy_to != gy) | (x != gy // 2))
            def _():
                copy(4, soft_mid, attn_recv.at[x], place(gy // 2, y, z), gy_to)

            return carry

        lax.fori_loop(0, 8, to_outputs, 0, unroll=True)

    @pl.when(source_gy == gy)
    def _():
        attn_recv[x] = soft_mid[...]
        await_bytes(attn_recv.at[pl.ds(0, 3)], recv_sem.at[4])

    @pl.when(source_gy != gy)
    def _():
        await_bytes(attn_recv, recv_sem.at[4])

    soft_wide[:4] = attn_recv[...].astype(jnp.float32)
    accum, _, _, columns = merge_partials(soft_wide, 4)
    attention = (accum[:PAIR] / columns[:PAIR, 4:5]).astype(jnp.bfloat16)
    attention = jnp.concatenate([attention[:ROWS], attention[ROWS:]], axis=1)
    loads[7].wait()
    out_part = jnp.dot(attention, w_output[...], preferred_element_type=jnp.float32)
    for j in range(SLICES):
        out_send[j, :ROWS, :] = out_part[:, j * 2 * HD : (j * 2 + 1) * HD]
        out_send[j, ROWS:, :] = out_part[:, (j * 2 + 1) * HD : (j * 2 + 2) * HD]

        @pl.when(j != plane)
        def _():
            copy(5, out_send.at[j], out_plane.at[plane], place(j // 2, y, j % 2), gy)

    all_reduce(5, out_send, out_plane, out_mid, out_line, out_sum, out_all)
    for j in range(SLICES):
        out_ref[:, j * 2 * HD : (j * 2 + 1) * HD] = out_all[j, :ROWS, :]
        out_ref[:, (j * 2 + 1) * HD : (j * 2 + 2) * HD] = out_all[j, ROWS:, :]

    for stage in range(3):
        await_bytes(in_all.at[pl.ds(0, 7)], send_sem.at[stage])
        await_bytes(out_all.at[pl.ds(0, 7)], send_sem.at[5 + stage])

    @pl.when(merges)
    def _():
        await_bytes(soft_recv.at[pl.ds(0, 7)], send_sem.at[3])

    @pl.when(jnp.logical_not(merges))
    def _():
        await_bytes(soft_recv.at[pl.ds(0, 8)], send_sem.at[3])

    @pl.when(merges & (x == gy // 2))
    def _():
        await_bytes(soft_recv.at[pl.ds(0, 7)], send_sem.at[4])

    @pl.when(merges & (x != gy // 2))
    def _():
        await_bytes(soft_recv.at[pl.ds(0, 8)], send_sem.at[4])


def per_device(hidden_in, norm_gain, w_query, w_keyval, w_output, key_cache, value_cache, lengths):
    hbm = pl.BlockSpec(memory_space=pltpu.HBM)

    def reduction(rows):
        return [
            pltpu.VMEM((SLICES, rows, HD), jnp.float32),
            pltpu.VMEM((SLICES, rows, HD), jnp.float32),
            pltpu.VMEM((rows, HD), jnp.float32),
            pltpu.VMEM((SLICES, rows, HD), jnp.float32),
            pltpu.VMEM((rows, HD), jnp.float32),
            pltpu.VMEM((SLICES, rows, HD), jnp.float32),
        ]

    scratch = [
        pltpu.VMEM(hidden_in.shape, jnp.bfloat16),
        pltpu.VMEM(norm_gain.shape, jnp.bfloat16),
        pltpu.VMEM(w_query.shape, jnp.bfloat16),
        pltpu.VMEM(w_keyval.shape, jnp.bfloat16),
        pltpu.VMEM(w_output.shape, jnp.bfloat16),
        pltpu.VMEM(key_cache.shape, jnp.bfloat16),
        pltpu.VMEM(value_cache.shape, jnp.bfloat16),
        pltpu.SMEM(lengths.shape, jnp.int32),
        pltpu.VMEM((ROWS, HD, SPAN), jnp.bfloat16),
        *reduction(BLOCK),
        pltpu.VMEM((16, SOFT, HD), jnp.float32),
        pltpu.VMEM((SLICES, SOFT, HD), jnp.bfloat16),
        pltpu.VMEM((16, SOFT, HD), jnp.bfloat16),
        pltpu.VMEM((SOFT, HD), jnp.bfloat16),
        pltpu.VMEM((4, SOFT, HD), jnp.bfloat16),
        *reduction(PAIR),
        pltpu.SemaphoreType.DMA((9,)),
        pltpu.SemaphoreType.DMA((8,)),
        pltpu.SemaphoreType.DMA((8,)),
        pltpu.SemaphoreType.REGULAR,
    ]
    out = pl.pallas_call(
        kernel,
        out_shape=jax.ShapeDtypeStruct((ROWS, GROUP * HD), jnp.float32),
        in_specs=[hbm] * 8,
        out_specs=pl.BlockSpec(memory_space=pltpu.VMEM),
        scratch_shapes=scratch,
        compiler_params=pltpu.CompilerParams(
            collective_id=0, has_side_effects=True, vmem_limit_bytes=16 * 2**20
        ),
    )(*[pltpu.with_memory_space_constraint(a, pltpu.HBM) for a in (hidden_in, norm_gain, w_query, w_keyval, w_output, key_cache, value_cache, lengths)])
    return out.astype(jnp.bfloat16)


def solution(mesh):
    return jax.shard_map(
        per_device,
        mesh=mesh,
        in_specs=(
            P(None, "gx"),
            P("gx"),
            P("gx", "gy"),
            P("gx", "gy"),
            P("gx", "gy"),
            P(None, "gy", "gx", None),
            P(None, "gy", "gx", None),
            P(),
        ),
        out_specs=P(None, "gy"),
        check_vma=False,
    )
```

```python
import jax
import jax.numpy as jnp
from jax import lax
from jax.experimental import pallas as pl
from jax.experimental.pallas import tpu as pltpu
from jax.sharding import PartitionSpec as P

D = 16384
HEADS = 128
KV = 8
HD = 128
ROWS = 10
GROUP = HEADS // KV
SPAN = 512
MESH = pl.DeviceIdType.MESH

SLICES = 8
PAIR = 2 * ROWS
BLOCK = PAIR + 4
SOFT = 32
PEAK = PAIR
TOTAL = PEAK + 3


def offset(index, size):
    return size // 2 + (1 - 2 * (index % 2)) * ((index + 1) // 2)


def await_bytes(ref, sem):
    pltpu.make_async_copy(ref, ref, sem).wait()


def split(value):
    high = value.astype(jnp.bfloat16).astype(jnp.float32)
    rest = value - high
    middle = rest.astype(jnp.bfloat16).astype(jnp.float32)
    return high, middle, rest - middle


def merge_partials(blocks, count):
    def joined(row):
        return blocks[:count, row, :] + blocks[:count, row + 1, :] + blocks[:count, row + 2, :]

    peaks = joined(PEAK)
    peak = jnp.max(peaks, axis=0, keepdims=True)
    factors = jnp.exp(peaks - peak)
    total = jnp.sum(factors * joined(TOTAL), axis=0, keepdims=True)
    if count < 8:
        factors = jnp.concatenate([factors, jnp.broadcast_to(total, (8 - count, HD))], axis=0)
    columns = jnp.transpose(factors)
    accum = columns[:BLOCK, 0:1] * blocks[0, :BLOCK]
    for k in range(1, count):
        accum = accum + columns[:BLOCK, k : k + 1] * blocks[k, :BLOCK]
    return accum, peak, total, columns


def kernel(
    hidden_hbm, gain_hbm, w_query_hbm, w_keyval_hbm, w_output_hbm, key_hbm, value_hbm, lengths_hbm,
    out_ref,
    hidden_in, norm_gain, w_query, w_keyval, w_output, keys, values, lengths, keys_across,
    in_send, in_plane, in_mid, in_line, in_sum, in_all,
    soft_wide, soft_send, soft_recv, soft_mid, attn_recv,
    out_send, out_plane, out_mid, out_line, out_sum,
    load_sem, send_sem, recv_sem, late_sem,
):
    gx, gy = lax.axis_index("gx"), lax.axis_index("gy")
    x, y, z = gx // 16, (gx // 2) % 8, gx % 2
    plane = x * 2 + z
    merges = y // 4 == gy % 2
    source_gy = 2 * x + y // 4

    def is_late(y):
        return (y + 5) % 8 < 4

    def place(x, y, z):
        return x * 16 + y * 2 + z

    def plane_mate(index):
        return (x + offset(index // 2, 4)) % 4, (z + 1 - index % 2) % 2

    def line_mate(index):
        return (y + offset(index, 8)) % 8

    loads = [
        pltpu.make_async_copy(src, dst, load_sem.at[k])
        for k, (src, dst) in enumerate(
            [
                (hidden_hbm, hidden_in),
                (gain_hbm, norm_gain),
                (w_query_hbm.at[:, pl.ds(0, 1024)], w_query.at[:, pl.ds(0, 1024)]),
                (w_query_hbm.at[:, pl.ds(1024, 1024)], w_query.at[:, pl.ds(1024, 1024)]),
                (w_keyval_hbm, w_keyval),
                (key_hbm, keys),
                (value_hbm, values),
                (w_output_hbm, w_output),
                (lengths_hbm, lengths),
            ]
        )
    ]

    barrier = pltpu.get_barrier_semaphore()

    def signal(gx_to, gy_to):
        pl.semaphore_signal(barrier, inc=1, device_id=(gx_to, gy_to), device_id_type=MESH)

    @pl.when(source_gy != gy)
    def _():
        signal(gx, source_gy)

    for index in range(7):
        x_mate, z_mate = plane_mate(index)
        signal(place(x_mate, y, z_mate), gy)
    for index in range(7):
        y_mate = line_mate(index)

        @pl.when(is_late(y_mate) | jnp.logical_not(is_late(y)))
        def _():
            signal(place(x, y_mate, z), gy)

    for load in loads[:5]:
        load.start()

    def copy(stage, src, dst, gx_to, gy_to):
        pltpu.make_async_remote_copy(
            src_ref=src, dst_ref=dst, send_sem=send_sem.at[stage], recv_sem=recv_sem.at[stage],
            device_id=(gx_to, gy_to), device_id_type=MESH,
        ).start()

    def all_reduce(stage, send, by_plane, mid, by_line, total, everything):
        if stage == 0:

            def to_plane(index, carry):
                x_mate, z_mate = plane_mate(index)
                copy(stage, send.at[x_mate * 2 + z_mate], by_plane.at[plane], place(x_mate, y, z_mate), gy)
                return carry

            lax.fori_loop(0, 7, to_plane, 0, unroll=True)
        if stage == 0:
            for load in loads[5:]:
                load.start()
        by_plane[plane] = send[plane]
        await_bytes(by_plane.at[pl.ds(0, 7)], recv_sem.at[stage])
        mid[...] = jnp.sum(by_plane[...], axis=0)
        if stage == 0:

            @pl.when(jnp.logical_not(is_late(y)))
            def _():
                pl.semaphore_wait(late_sem, 4)

        def to_line(index, carry):
            copy(stage + 1, mid, by_line.at[y], place(x, line_mate(index), z), gy)
            return carry

        lax.fori_loop(0, 7, to_line, 0, unroll=True)
        if stage == 0:
            loads[5].wait()
            for r in range(ROWS):
                keys_across[r] = jnp.transpose(keys[r, 0])
        by_line[y] = mid[...]
        await_bytes(by_line.at[pl.ds(0, 7)], recv_sem.at[stage + 1])
        summed = jnp.sum(by_line[...], axis=0)
        if stage == 0:
            total[...] = summed
        else:
            total[:, :HD] = summed[:ROWS]
            total[:, HD:] = summed[ROWS:]

        def slice_of(ref):
            if stage == 0:
                return ref.at[plane]
            return ref.at[:, pl.ds(pl.multiple_of(plane * 2 * HD, 2 * HD), 2 * HD)]

        def mates_of(ref):
            return ref.at[pl.ds(0, 7)] if stage == 0 else ref.at[:, pl.ds(0, 7 * 2 * HD)]


        def back_to_plane(index, carry):
            x_mate, z_mate = plane_mate(index)
            copy(stage + 2, total, slice_of(everything), place(x_mate, y, z_mate), gy)
            return carry

        lax.fori_loop(0, 7, back_to_plane, 0, unroll=True)
        slice_of(everything)[...] = total[...]
        await_bytes(mates_of(everything), recv_sem.at[stage + 2])

    loads[0].wait()
    loads[1].wait()
    hidden = hidden_in[...].astype(jnp.float32)
    squares = jnp.broadcast_to(jnp.sum(hidden * hidden, axis=1, keepdims=True), (ROWS, HD))
    gain = norm_gain[...].astype(jnp.float32).reshape(1, -1)
    scaled_in = (hidden * gain).astype(jnp.bfloat16)
    for part in range(2):
        loads[2 + part].wait()
        columns = slice(part * 1024, (part + 1) * 1024)
        query_part = jnp.dot(scaled_in, w_query[:, columns], preferred_element_type=jnp.float32)
        for k in range(4):
            j = part * 4 + k
            in_send[j, :ROWS, :] = query_part[:, k * 2 * HD : (k * 2 + 1) * HD]
            in_send[j, ROWS:PAIR, :] = query_part[:, (k * 2 + 1) * HD : (k * 2 + 2) * HD]
    loads[4].wait()
    keyval_part = jnp.dot(scaled_in, w_keyval[...], preferred_element_type=jnp.float32)
    extras = [keyval_part[:, :HD], keyval_part[:, HD:], squares, jnp.zeros((2, HD), jnp.float32)]
    slot = 0
    for extra in extras:
        for r in range(extra.shape[0]):
            in_send[slot // 4, PAIR + slot % 4 : PAIR + slot % 4 + 1, :] = extra[r : r + 1]
            slot += 1

    greetings = 10 + 4 * is_late(y).astype(jnp.int32) + 7 * (source_gy == gy).astype(jnp.int32)
    pl.semaphore_wait(barrier, greetings)

    @pl.when(is_late(y))
    def _():
        for y_mate in (0, 1, 7, 2):
            pl.semaphore_signal(
                late_sem, inc=1, device_id=(place(x, y_mate, z), gy), device_id_type=MESH
            )

    all_reduce(0, in_send, in_plane, in_mid, in_line, in_sum, in_all)

    def extra_row(kind, r):
        slot = kind * ROWS + r
        return in_all[slot // 4, PAIR + slot % 4 : PAIR + slot % 4 + 1, :]

    loads[8].wait()
    score_scale = HD ** (-0.5)
    position = gx * SPAN + lax.broadcasted_iota(jnp.int32, (GROUP, SPAN), 1)
    first = gx == 0
    queries, scores, values_new, scores_new = [], [], [], []
    for r in range(ROWS):
        inv_rms = lax.rsqrt(extra_row(2, r) / D + 1e-05)
        query = jnp.concatenate([in_all[:, r, :], in_all[:, ROWS + r, :]], axis=0)
        query = (query * inv_rms).astype(jnp.bfloat16)
        key_new = (extra_row(0, r) * inv_rms).astype(jnp.bfloat16).astype(jnp.float32)
        values_new.append((extra_row(1, r) * inv_rms).astype(jnp.bfloat16).astype(jnp.float32))
        score_new = (
            jnp.sum(query.astype(jnp.float32) * key_new, axis=1, keepdims=True) * score_scale
        )
        scores_new.append(jnp.where(first, score_new, -1e30))
        scores.append(
            jnp.dot(query, keys_across[r], preferred_element_type=jnp.float32)
            * score_scale
        )
    loads[6].wait()
    head_row = lax.broadcasted_iota(jnp.int32, (GROUP, HD), 0)
    lane = lax.broadcasted_iota(jnp.int32, (GROUP, HD), 1) - ROWS * (head_row // SLICES)
    peaks = jnp.zeros((GROUP, HD), jnp.float32)
    totals = jnp.zeros((GROUP, HD), jnp.float32)
    for r in range(ROWS):
        valid = position < lengths[r]
        masked = jnp.where(valid, scores[r], -1e30)
        peak = jnp.maximum(jnp.max(masked, axis=1, keepdims=True), scores_new[r])
        peak = jnp.maximum(peak, -1e29)
        weights = jnp.exp(masked - peak)
        fresh = jnp.where(first, jnp.exp(scores_new[r] - peak), 0.0)
        total = jnp.sum(weights, axis=1, keepdims=True) + fresh
        accum = jnp.dot(
            weights.astype(jnp.bfloat16), values[r, 0], preferred_element_type=jnp.float32
        )
        accum = accum + fresh * values_new[r]
        soft_wide[:SLICES, r, :] = accum[:SLICES]
        soft_wide[:SLICES, ROWS + r, :] = accum[SLICES:]
        peaks = jnp.where(lane == r, peak, peaks)
        totals = jnp.where(lane == r, total, totals)
    terms = split(peaks[:SLICES] + peaks[SLICES:]) + split(totals[:SLICES] + totals[SLICES:])
    for k in range(SOFT - PEAK):
        term = terms[k] if k < 6 else jnp.zeros((SLICES, HD), jnp.float32)
        soft_wide[:SLICES, PEAK + k, :] = term
    soft_send[...] = soft_wide[:SLICES].astype(jnp.bfloat16)

    for index in range(8):
        y_to = (y + offset(index, 8)) % 8
        for z_step in (1, 0):
            if index == 7 and z_step == 0:
                continue
            z_to = (z + z_step) % 2

            @pl.when(y_to // 4 == gy % 2)
            def _():
                copy(3, soft_send.at[(y_to % 4) * 2 + z_to], soft_recv.at[y * 2 + z], place(x, y_to, z_to), gy)

    @pl.when(merges)
    def _():
        soft_recv[y * 2 + z] = soft_send[(y % 4) * 2 + z]
        await_bytes(soft_recv.at[pl.ds(0, 15)], recv_sem.at[3])
        soft_wide[...] = soft_recv[...].astype(jnp.float32)
        accum, peak, total, _ = merge_partials(soft_wide, 16)
        merged = soft_wide.at[0]
        merged[:BLOCK, :] = accum
        merged[BLOCK:, :] = jnp.zeros((SOFT - BLOCK, HD), jnp.float32)
        for k, term in enumerate(split(peak) + split(total)):
            merged[PEAK + k : PEAK + k + 1, :] = term
        soft_mid[...] = merged[...].astype(jnp.bfloat16)

        def to_outputs(index, carry):
            gy_to = index

            @pl.when((gy_to != gy) | (x != gy // 2))
            def _():
                copy(4, soft_mid, attn_recv.at[x], place(gy // 2, y, z), gy_to)

            return carry

        lax.fori_loop(0, 8, to_outputs, 0, unroll=True)

    @pl.when(source_gy == gy)
    def _():
        attn_recv[x] = soft_mid[...]
        await_bytes(attn_recv.at[pl.ds(0, 3)], recv_sem.at[4])

    @pl.when(source_gy != gy)
    def _():
        await_bytes(attn_recv, recv_sem.at[4])

    soft_wide[:4] = attn_recv[...].astype(jnp.float32)
    accum, _, _, columns = merge_partials(soft_wide, 4)
    attention = (accum[:PAIR] / columns[:PAIR, 4:5]).astype(jnp.bfloat16)
    attention = jnp.concatenate([attention[:ROWS], attention[ROWS:]], axis=1)
    loads[7].wait()
    out_part = jnp.dot(attention, w_output[...], preferred_element_type=jnp.float32)
    for j in range(SLICES):
        out_send[j, :ROWS, :] = out_part[:, j * 2 * HD : (j * 2 + 1) * HD]
        out_send[j, ROWS:, :] = out_part[:, (j * 2 + 1) * HD : (j * 2 + 2) * HD]

        @pl.when(j != plane)
        def _():
            copy(5, out_send.at[j], out_plane.at[plane], place(j // 2, y, j % 2), gy)

    all_reduce(5, out_send, out_plane, out_mid, out_line, out_sum, out_ref)

    for stage in range(3):
        await_bytes(in_all.at[pl.ds(0, 7)], send_sem.at[stage])
        sent = out_line.at[pl.ds(0, 7)] if stage < 2 else out_ref.at[:, pl.ds(0, 7 * 2 * HD)]
        await_bytes(sent, send_sem.at[5 + stage])

    @pl.when(merges)
    def _():
        await_bytes(soft_recv.at[pl.ds(0, 7)], send_sem.at[3])

    @pl.when(jnp.logical_not(merges))
    def _():
        await_bytes(soft_recv.at[pl.ds(0, 8)], send_sem.at[3])

    @pl.when(merges & (x == gy // 2))
    def _():
        await_bytes(soft_recv.at[pl.ds(0, 7)], send_sem.at[4])

    @pl.when(merges & (x != gy // 2))
    def _():
        await_bytes(soft_recv.at[pl.ds(0, 8)], send_sem.at[4])


def per_device(hidden_in, norm_gain, w_query, w_keyval, w_output, key_cache, value_cache, lengths):
    hbm = pl.BlockSpec(memory_space=pltpu.HBM)

    def reduction(rows):
        return [
            pltpu.VMEM((SLICES, rows, HD), jnp.float32),
            pltpu.VMEM((SLICES, rows, HD), jnp.float32),
            pltpu.VMEM((rows, HD), jnp.float32),
            pltpu.VMEM((SLICES, rows, HD), jnp.float32),
            pltpu.VMEM((rows, HD), jnp.float32),
            pltpu.VMEM((SLICES, rows, HD), jnp.float32),
        ]

    scratch = [
        pltpu.VMEM(hidden_in.shape, jnp.bfloat16),
        pltpu.VMEM(norm_gain.shape, jnp.bfloat16),
        pltpu.VMEM(w_query.shape, jnp.bfloat16),
        pltpu.VMEM(w_keyval.shape, jnp.bfloat16),
        pltpu.VMEM(w_output.shape, jnp.bfloat16),
        pltpu.VMEM(key_cache.shape, jnp.bfloat16),
        pltpu.VMEM(value_cache.shape, jnp.bfloat16),
        pltpu.SMEM(lengths.shape, jnp.int32),
        pltpu.VMEM((ROWS, HD, SPAN), jnp.bfloat16),
        *reduction(BLOCK),
        pltpu.VMEM((16, SOFT, HD), jnp.float32),
        pltpu.VMEM((SLICES, SOFT, HD), jnp.bfloat16),
        pltpu.VMEM((16, SOFT, HD), jnp.bfloat16),
        pltpu.VMEM((SOFT, HD), jnp.bfloat16),
        pltpu.VMEM((4, SOFT, HD), jnp.bfloat16),
        *reduction(PAIR)[:4],
        pltpu.VMEM((ROWS, 2 * HD), jnp.float32),
        pltpu.SemaphoreType.DMA((9,)),
        pltpu.SemaphoreType.DMA((8,)),
        pltpu.SemaphoreType.DMA((8,)),
        pltpu.SemaphoreType.REGULAR,
    ]
    out = pl.pallas_call(
        kernel,
        out_shape=jax.ShapeDtypeStruct((ROWS, GROUP * HD), jnp.float32),
        in_specs=[hbm] * 8,
        out_specs=pl.BlockSpec(memory_space=pltpu.VMEM),
        scratch_shapes=scratch,
        compiler_params=pltpu.CompilerParams(
            collective_id=0, has_side_effects=True, vmem_limit_bytes=16 * 2**20
        ),
    )(*[pltpu.with_memory_space_constraint(a, pltpu.HBM) for a in (hidden_in, norm_gain, w_query, w_keyval, w_output, key_cache, value_cache, lengths)])
    return out.astype(jnp.bfloat16)


def solution(mesh):
    return jax.shard_map(
        per_device,
        mesh=mesh,
        in_specs=(
            P(None, "gx"),
            P("gx"),
            P("gx", "gy"),
            P("gx", "gy"),
            P("gx", "gy"),
            P(None, "gy", "gx", None),
            P(None, "gy", "gx", None),
            P(),
        ),
        out_specs=P(None, "gy"),
        check_vma=False,
    )
```
